128 devices in a mesh: node: 8 (over z_lo, y), local: 16 (over x, z_hi, core).
Axes of the slice: x: 4, y: 4, z: 4 (z_hi: 2, z_lo: 2; z = z_hi * 2 + z_lo), core: 2. Of those that a mesh axis runs over, the one named last changes fastest.
Arguments:
- cache_pool: bfloat16 [512, 576, 256], P(('node', 'local')), may hold values from -6 to 6
- block_table: int32 [256, 2], P(('node', 'local')), may hold values from 0 to 3, as said below
- lengths: int32 [256], replicated, may hold values from 128 to 512
- mig_slot: int32 [128], replicated, may hold values from 0 to 1
- mig_dest: int32 [128], replicated, may hold values from 0 to 127, each once
- queries: bfloat16 [3, 256, 73728], P(None, ('node', 'local'))
- new_entries: bfloat16 [3, 256, 576], P(None, ('node', 'local')), may hold values from -6 to 6
- residual: bfloat16 [3, 256, 7168], P(None, None, 'node'), may hold values from -0.75 to 0.75
- w_uv: bfloat16 [128, 512, 128], P('local'), may hold values from -0.25 to 0.25
- w_out: bfloat16 [16384, 7168], P('local', 'node'), may hold values from -0.046875 to 0.046875
- norm_gain: float32 [7168], P('node'), may hold values from 0.1 to 1.9
- w_gate: bfloat16 [7168, 18432], P('node', 'local'), may hold values from -0.0625 to 0.0625
- w_up: bfloat16 [7168, 18432], P('node', 'local'), may hold values from -0.0625 to 0.0625
- w_down: bfloat16 [18432, 7168], P('local', 'node'), may hold values from -0.046875 to 0.046875
Outputs:
- layer_out: bfloat16 [3, 256, 7168], P(None, 'local', 'node')
The draws below stay inside these ranges and needn't reach their ends.
Inputs may be any that keep to these rules, and one draw needn't show every extreme that they name: `block_table`: the 2 rows of one device name each of its 4 pool blocks once. `mig_dest`: every device is the destination of exactly one device, possibly itself.
All inputs are finite; a program needn't handle non-finite values.
Results may differ from the reference program's by a relative error of at most 0.035.
Values may be sent and summed in bfloat16 or wider, within the bound.
A program may use at most 128 MiB of HBM per device.

```python
import jax
import jax.numpy as jnp
from jax import lax

D = 7168
FF = 18432
H = 128
LATENT = 512
ROPE = 64
QK_NOPE = 128
V_DIM = 128
BLOCK = 256
MAXB = 2
STEPS = 3
REQ_DEV = 2
POOL = 4
REQS = 256
N_NODE = 8
N_LOCAL = 16
DEVICES = 128


def draw_block_table(key, part):
    key = jax.random.fold_in(key, 5)
    device_count = REQS // REQ_DEV
    device_keys = jax.random.split(key, device_count)
    orders = jax.vmap(lambda single_key: jax.random.permutation(single_key, POOL))(device_keys)
    return orders.reshape(REQS, MAXB).astype(jnp.int32)


def draw_lengths(key, part):
    key = jax.random.fold_in(key, 11)
    drawn = jax.random.randint(key, (REQS,), BLOCK // 2, MAXB * BLOCK + 1)
    drawn = drawn.at[0].set(MAXB * BLOCK)
    drawn = drawn.at[1].set(BLOCK // 2)
    return drawn.astype(jnp.int32)


def draw_queries(key, part):
    key = jax.random.fold_in(key, 7)
    value_key = jax.random.fold_in(key, 0)
    shape = (STEPS, REQS, H, LATENT + ROPE)
    drawn = jax.random.normal(value_key, shape, jnp.float32)
    return drawn.reshape(STEPS, REQS, H * (LATENT + ROPE)).astype(jnp.bfloat16)


def plant(result, key, low, top_value):
    extent = result.shape
    spot = [jax.random.randint(jax.random.fold_in(key, axis), (), 0, extent[axis]) for axis in range(len(extent))]
    result = result.at[tuple(spot)].set(low)
    longest = extent.index(max(extent))
    spot[longest] = (spot[longest] + 1) % extent[longest]
    return result.at[tuple(spot)].set(top_value)


def shard_levels(own_key, extent, cuts, low, high):
    gain = 1.0
    for dim, blocks in cuts:
        steps = jax.random.uniform(jax.random.fold_in(jax.random.fold_in(own_key, 6), dim), (blocks,), jnp.float32, low / len(cuts), high / len(cuts))
        gain = gain * jnp.repeat(jnp.exp(steps), extent[dim] // blocks).reshape((-1,) + (1,) * (len(extent) - 1 - dim))
    return gain


def noise(own_key, dims, deviation, most, cuts=(), kind=jnp.bfloat16):
    values = deviation * jax.random.normal(own_key, dims, jnp.float32)
    if cuts:
        values = values * shard_levels(own_key, dims, cuts, -0.22, 0.18)
    return jnp.clip(values, -most, most).astype(kind)


def setup_inputs(seed: int = 0) -> dict:
    key_of = jax.random.split(jax.random.key(seed), 15)
    return {
        "cache_pool": noise(key_of[0], (DEVICES * POOL, LATENT + ROPE, BLOCK), 1.0, 6.0, ((0, 128),)),
        "block_table": draw_block_table(jax.random.fold_in(key_of[14], 71), 0),
        "lengths": draw_lengths(jax.random.fold_in(key_of[14], 71), 0),
        "mig_slot": plant(jax.random.randint(key_of[3], (DEVICES,), 0, REQ_DEV), jax.random.fold_in(key_of[3], 1), 0, REQ_DEV - 1).astype(jnp.int32),
        "mig_dest": jax.random.permutation(key_of[4], DEVICES).astype(jnp.int32),
        "queries": draw_queries(jax.random.fold_in(key_of[14], 71), 0),
        "new_entries": noise(key_of[6], (STEPS, REQS, LATENT + ROPE), 1.0, 6.0, ((1, 128),)),
        "residual": noise(key_of[7], (STEPS, REQS, D), 0.05, 0.75, ((2, 8),)),
        "w_uv": noise(key_of[8], (H, LATENT, V_DIM), LATENT ** -0.5, 0.25, ((0, 16),)),
        "w_out": noise(key_of[9], (H * V_DIM, D), (H * V_DIM) ** -0.5, 0.046875, ((0, 16), (1, 8))),
        "norm_gain": jnp.clip(1.0 + 0.18 * jax.random.normal(key_of[10], (D,), jnp.float32), 0.1, 1.9),
        "w_gate": noise(key_of[11], (D, FF), D ** -0.5, 0.0625, ((0, 8), (1, 16))),
        "w_up": noise(key_of[12], (D, FF), D ** -0.5, 0.0625, ((0, 8), (1, 16))),
        "w_down": noise(key_of[13], (FF, D), FF ** -0.5, 0.046875, ((0, 16), (1, 8))),
    }


epsilon = 1e-06

def rounded(values):
    return lax.optimization_barrier(values.astype(jnp.bfloat16)).astype(jnp.float32)

def attend(queries_now, caches, lengths_now, fresh_keys, score_scale):
    query_wide = queries_now.astype(jnp.float32)
    cache_wide = caches.astype(jnp.float32)
    fresh_wide = fresh_keys.astype(jnp.float32)
    blocks = caches.shape[1]
    columns = caches.shape[3]
    scores = jnp.einsum('rhc,rbct->rhbt', query_wide, cache_wide) * score_scale
    position = lax.broadcasted_iota(jnp.int32, (blocks, columns), 0) * columns + lax.broadcasted_iota(jnp.int32, (blocks, columns), 1)
    visible = position[None, :, :] < lengths_now[:, None, None]
    scores = jnp.where(visible[:, None, :, :], scores, -jnp.inf)
    fresh_scores = jnp.einsum('rhc,nrc->rhn', query_wide, fresh_wide) * score_scale
    highest = jnp.maximum(lax.optimization_barrier(jnp.max(scores, axis=(2, 3))), lax.optimization_barrier(jnp.max(fresh_scores, axis=2)))
    cache_weights = jnp.exp(scores - highest[:, :, None, None])
    fresh_weights = jnp.exp(fresh_scores - highest[:, :, None])
    totals = lax.optimization_barrier(jnp.sum(cache_weights, axis=(2, 3))) + lax.optimization_barrier(jnp.sum(fresh_weights, axis=2))
    cache_weights = rounded(cache_weights / totals[:, :, None, None])
    fresh_weights = rounded(fresh_weights / totals[:, :, None])
    context = jnp.einsum('rhbt,rbct->rhc', cache_weights, cache_wide[:, :, :LATENT, :])
    context = context + jnp.einsum('rhn,nrc->rhc', fresh_weights, fresh_wide[:, :, :LATENT])
    return context.astype(jnp.bfloat16)

def reference(cache_pool, block_table, lengths, mig_slot, mig_dest, queries, new_entries, residual, w_uv, w_out, norm_gain, w_gate, w_up, w_down):
    devices = N_NODE * N_LOCAL
    entry_width = LATENT + ROPE
    score_scale = (QK_NOPE + ROPE) ** (-0.5)
    pools = cache_pool.reshape(devices, POOL, entry_width, BLOCK)
    tables = block_table.reshape(devices, REQ_DEV, MAXB)
    owner_lengths = lengths.reshape(devices, REQ_DEV)
    anchors = jnp.zeros((devices,), jnp.int32).at[mig_dest].set(jnp.arange(devices, dtype=jnp.int32))
    anchor_slots = mig_slot[anchors]
    is_leaving = jnp.arange(REQ_DEV, dtype=jnp.int32)[None, :] == mig_slot[:, None]
    arrival_lengths = owner_lengths[anchors, anchor_slots]
    serve_lengths = jnp.where(is_leaving, arrival_lengths[:, None], owner_lengths)
    step_queries = queries.reshape(STEPS, devices, REQ_DEV, H, entry_width)
    fresh_all = new_entries.reshape(STEPS, devices, REQ_DEV, entry_width)

    def one_device(device):
        owned = pools[device][tables[device]]
        source = anchors[device]
        arrival = pools[source][tables[source, anchor_slots[device]]]
        serving = jnp.where(is_leaving[device][:, None, None, None], arrival[None], owned)
        results = []
        for step_index in range(STEPS):
            results.append(attend(step_queries[step_index, device], serving, serve_lengths[device], fresh_all[:step_index + 1, device], score_scale))
        return jnp.stack(results)
    contexts = lax.map(one_device, jnp.arange(devices, dtype=jnp.int32))
    contexts = jnp.moveaxis(contexts, 1, 0).reshape(STEPS, REQS, H, LATENT)
    group_heads = H // N_LOCAL
    out_rows = w_out.reshape(N_LOCAL, group_heads * V_DIM, D).astype(jnp.float32)
    gate_rows = w_gate.reshape(N_NODE, D // N_NODE, FF).astype(jnp.float32)
    up_rows = w_up.reshape(N_NODE, D // N_NODE, FF).astype(jnp.float32)
    down_rows = w_down.reshape(N_LOCAL, FF // N_LOCAL, D).astype(jnp.float32)
    outputs = []
    for step_index in range(STEPS):
        values = rounded(jnp.einsum('rhc,hcv->rhv', contexts[step_index].astype(jnp.float32), w_uv.astype(jnp.float32)))
        grouped = values.reshape(REQS, N_LOCAL, group_heads * V_DIM)
        attn_out = lax.optimization_barrier(jnp.sum(rounded(jnp.einsum('rgk,gkd->grd', grouped, out_rows)), axis=0))
        mixed = rounded(residual[step_index].astype(jnp.float32) + attn_out)
        inverse = lax.rsqrt(lax.optimization_barrier(jnp.mean(mixed * mixed, axis=1)) + epsilon)
        normed = rounded(mixed * inverse[:, None] * norm_gain.astype(jnp.float32)[None, :])
        pieces = normed.reshape(REQS, N_NODE, D // N_NODE)
        gate = lax.optimization_barrier(jnp.sum(rounded(jnp.einsum('rnd,ndf->nrf', pieces, gate_rows)), axis=0))
        upward = lax.optimization_barrier(jnp.sum(rounded(jnp.einsum('rnd,ndf->nrf', pieces, up_rows)), axis=0))
        hidden = rounded(jax.nn.silu(gate) * upward)
        block_out = lax.optimization_barrier(jnp.sum(rounded(jnp.einsum('rgf,gfd->grd', hidden.reshape(REQS, N_LOCAL, FF // N_LOCAL), down_rows)), axis=0))
        outputs.append((mixed + block_out).astype(jnp.bfloat16))
    return jnp.stack(outputs)
```

```python
import functools

import jax
import jax.numpy as jnp
from jax import lax
from jax.experimental import pallas as pl
from jax.experimental.pallas import tpu as pltpu
from jax.sharding import PartitionSpec as P

MESH = pl.DeviceIdType.MESH
BF16, F32 = jnp.bfloat16, jnp.float32
D = 7168
QK_NOPE = 128
LATENT = 512
ROPE = 64
WIDTH = LATENT + ROPE
STEPS = 3
HEADS = 128
NODES, LOCALS = 8, 16
DEVS = NODES * LOCALS
CHIPS = LOCALS // 2
TILES = 128
EPS = 1e-06
SCALE = (QK_NOPE + ROPE) ** (-0.5)
NODE_ROWS = 96
SHARE = 48
COLS = 896
HID = 1152
NT = (((1,), (1,)), ((), ()))


def dot(a, b):
    return jnp.dot(a, b, preferred_element_type=F32)


def dot_nt(a, b):
    return lax.dot_general(a, b, NT, preferred_element_type=F32)


def rcopy(src, dst, send, recv, device):
    return pltpu.make_async_remote_copy(
        src_ref=src, dst_ref=dst, send_sem=send, recv_sem=recv, device_id=device, device_id_type=MESH
    )


def attend(query, fresh, key0, key1, length):
    s0 = dot(query, key0) * SCALE
    s1 = dot(query, key1) * SCALE
    sf = dot_nt(query, fresh) * SCALE
    rows, block = s0.shape
    column = lax.broadcasted_iota(jnp.int32, (rows, block), 1)
    s0 = jnp.where(column < length, s0, -jnp.inf)
    s1 = jnp.where(column + block < length, s1, -jnp.inf)
    step = lax.broadcasted_iota(jnp.int32, sf.shape, 0) // HEADS
    entry = lax.broadcasted_iota(jnp.int32, sf.shape, 1)
    sf = jnp.where(entry <= step, sf, -jnp.inf)
    top = jnp.maximum(
        jnp.max(jnp.maximum(s0, s1), axis=1, keepdims=True), jnp.max(sf, axis=1, keepdims=True)
    )
    w0 = jnp.exp(s0 - top)
    w1 = jnp.exp(s1 - top)
    wf = jnp.exp(sf - top)
    total = jnp.sum(w0 + w1, axis=1, keepdims=True) + jnp.sum(wf, axis=1, keepdims=True)
    context = dot_nt(w0.astype(BF16), key0[:LATENT])
    context += dot_nt(w1.astype(BF16), key1[:LATENT])
    context += dot(wf.astype(BF16), fresh[:, :LATENT])
    return context / total


def kernel(
    ints, tiles, query_stay, fresh_stay, pool, source, resid, gain,
    wuv_hbm, wout_hbm, wg_hbm, wu_hbm, wd_hbm,
    out,
    wuv, wout, wg, wu, wd,
    r1, s2, r2, query_arr, fresh_arr, ctx, ctx_send, ctx_recv, ctx_wide,
    values, proj, part, pair, share_send, share_recv, mixed,
    gu_send, gu_recv, sq_send, sq_recv, hidden,
    part2, pair2, share_send2, share_recv2,
    wsem, ready, sem, node_sem, local_sem, hid_sem, pair_sem, pair_sem2,
):
    n, l = lax.axis_index("node"), lax.axis_index("local")
    me = n * LOCALS + l
    core, chip = lax.rem(l, 2), l // 2
    sibling = (n, l + 1 - 2 * core)

    weights = [
        pltpu.make_async_copy(a, b, wsem.at[i])
        for i, (a, b) in enumerate(
            ((wuv_hbm, wuv), (wout_hbm, wout), (wg_hbm, wg), (wu_hbm, wu), (wd_hbm, wd))
        )
    ]
    for copy in weights:
        copy.start()

    barrier = pltpu.get_barrier_semaphore()

    def greet_node(i, c):
        pl.semaphore_signal(barrier, inc=1, device_id=(lax.rem(n + i, NODES), l), device_id_type=MESH)
        return c

    def greet_local(i, c):
        pl.semaphore_signal(barrier, inc=1, device_id=(n, lax.rem(l + i, LOCALS)), device_id_type=MESH)
        return c

    def greet_all(i, c):
        pl.semaphore_signal(ready, inc=1, device_id=(n, lax.rem(l + i, LOCALS)), device_id_type=MESH)
        return c

    lax.fori_loop(1, NODES, greet_node, 0)
    lax.fori_loop(1, LOCALS, greet_local, 0)
    pl.semaphore_wait(barrier, NODES - 1 + LOCALS - 1)
    lax.fori_loop(1, LOCALS, greet_all, 0)
    pl.semaphore_wait(ready, LOCALS - 1)

    def spread(i, c):
        p = lax.rem(me + i, DEVS)
        rcopy(tiles.at[p], r1.at[me], sem.at[0], sem.at[1], (p // LOCALS, lax.rem(p, LOCALS))).start()
        return c

    lax.fori_loop(1, DEVS, spread, 0)
    r1[me] = tiles[me]
    ctx[0] = attend(query_stay[...], fresh_stay[...], pool[ints[0]], pool[ints[1]], ints[4])
    both = pl.ds(0, DEVS - 1)
    rcopy(tiles.at[both], r1.at[both], sem.at[0], sem.at[1], (n, l)).wait()

    def sort(o, c):
        s2[o] = r1[ints[6 + o]]
        return c

    lax.fori_loop(0, DEVS, sort, 0)

    def deliver(i, c):
        p = lax.rem(me + i, DEVS)
        rcopy(s2.at[p], r2.at[me], sem.at[2], sem.at[3], (p // LOCALS, lax.rem(p, LOCALS))).start()
        return c

    lax.fori_loop(1, DEVS, deliver, 0)
    r2[me] = s2[me]
    rcopy(s2.at[both], r2.at[both], sem.at[2], sem.at[3], (n, l)).wait()
    for s in range(STEPS):
        for hb in range(HEADS // 16):
            for cb in range(5):
                query_arr[s * HEADS + hb * 16 : s * HEADS + hb * 16 + 16, cb * 128 : cb * 128 + 128] = r2[
                    (s * (HEADS // 16) + hb) * 5 + cb
                ]
    for cb in range(5):
        fresh_arr[:, cb * 128 : cb * 128 + 128] = r2[STEPS * (HEADS // 16) * 5 + cb]
    ctx[1] = attend(query_arr[:, :WIDTH], fresh_arr[:, :WIDTH], pool[ints[2]], pool[ints[3]], ints[5])

    def group(g):
        at = pl.multiple_of(g * 8, 8)
        pieces = [ctx[j, pl.ds(s * HEADS + at, 8), :] for j in range(2) for s in range(STEPS)]
        return jnp.concatenate(pieces, axis=0).astype(BF16)

    def send_group(i, c):
        g = lax.rem(l + i, LOCALS)
        ctx_send[g] = group(g)
        rcopy(ctx_send.at[g], ctx_recv.at[l], sem.at[4], sem.at[5], (n, g)).start()
        return c

    lax.fori_loop(1, LOCALS, send_group, 0)
    ctx_recv[l] = group(l)
    weights[0].wait()
    others = pl.ds(0, LOCALS - 1)
    rcopy(ctx_send.at[others], ctx_recv.at[others], sem.at[4], sem.at[5], (n, l)).wait()
    for t in range(LATENT // 128):
        ctx_wide[t] = ctx_recv[:, :, t * 128 : t * 128 + 128].reshape(LOCALS * SHARE, 128).astype(F32)
    for h in range(8):
        rows = [ctx_wide[t, pl.ds(h, NODE_ROWS, stride=8), :] for t in range(LATENT // 128)]
        rows = jnp.concatenate(rows, axis=1).astype(BF16)
        values[n, :, h * 128 : h * 128 + 128] = dot(rows, wuv[h]).astype(BF16)

    def send_values(i, c):
        p = lax.rem(n + i, NODES)
        rcopy(values.at[n], values.at[n], sem.at[6], node_sem.at[n], (p, l)).start()
        return c

    lax.fori_loop(1, NODES, send_values, 0)
    weights[1].wait()
    proj[n] = dot(values[n], wout[...]).astype(BF16)

    def project(i, c):
        p = lax.rem(n + NODES - i, NODES)
        rcopy(values.at[p], values.at[p], sem.at[6], node_sem.at[p], (n, l)).wait_recv()
        proj[p] = dot(values[p], wout[...]).astype(BF16)
        return c

    lax.fori_loop(1, NODES, project, 0)
    sent = pl.ds(0, NODES - 1)
    rcopy(values.at[sent], values.at[sent], sem.at[6], node_sem.at[0], (n, l)).wait_send()

    def scatter(make, part, pair, pair_sem, share_send, share_recv, send, recv):
        def produce(i, c):
            q = lax.rem(chip // 2 + i, 4)
            block = make(q).astype(BF16).reshape(4, SHARE, COLS)
            for k in range(4):
                part[k % 2, 2 * q + k // 2] = block[k]
            two = pl.ds(2 * q, 2)
            rcopy(part.at[1 - core, two], pair.at[two], send.at[0], pair_sem.at[q], sibling).start()
            return c

        lax.fori_loop(1, 5, produce, 0)

        def combine(i, c):
            q = lax.rem(chip // 2 + i, 4)
            two = pl.ds(2 * q, 2)
            rcopy(part.at[1 - core, two], pair.at[two], send.at[0], pair_sem.at[q], sibling).wait_recv()
            for k in range(2):
                to = 2 * q + k
                total = (part[core, to].astype(F32) + pair[to].astype(F32)).astype(BF16)

                @pl.when(to != chip)
                def _():
                    share_send[to] = total
                    rcopy(
                        share_send.at[to], share_recv.at[chip], send.at[1], recv, (n, to * 2 + core)
                    ).start()

                @pl.when(to == chip)
                def _():
                    share_recv[chip] = total

            return c

        lax.fori_loop(1, 5, combine, 0)
        rcopy(part.at[0], pair, send.at[0], pair_sem.at[0], sibling).wait_send()
        seven = pl.ds(0, CHIPS - 1)
        rcopy(share_send.at[seven], share_recv.at[seven], send.at[1], recv, sibling).wait()
        return jnp.sum(share_recv[...].astype(F32), axis=0)

    def permuted(q):
        rows = source[pl.ds(pl.multiple_of(q * 192, 192), 192), :]
        column = lax.broadcasted_iota(jnp.int32, (192, 768), 1)
        pick = jnp.where(rows == column, 1.0, 0.0).astype(BF16)
        return dot(pick, proj[...].reshape(768, COLS))

    attn = scatter(
        permuted, part, pair, pair_sem, share_send, share_recv, sem.at[pl.ds(8, 2)], sem.at[10]
    )
    mine = (resid[...].astype(F32) + attn).astype(BF16)
    mixed[l] = mine

    def send_mixed(i, c):
        to = lax.rem(chip + i, CHIPS)
        rcopy(mixed.at[l], mixed.at[l], sem.at[11], local_sem.at[l], (n, to * 2 + core)).start()
        return c

    lax.fori_loop(1, CHIPS, send_mixed, 0)
    rcopy(mixed.at[l], mixed.at[l], sem.at[12], local_sem.at[l], sibling).start()

    def pass_mixed(i, c):
        b = lax.rem(chip + CHIPS - i, CHIPS) * 2 + core
        rcopy(mixed.at[b], mixed.at[b], sem.at[11], local_sem.at[b], (n, l)).wait_recv()
        rcopy(mixed.at[b], mixed.at[b], sem.at[12], local_sem.at[b], sibling).start()
        return c

    lax.fori_loop(1, CHIPS, pass_mixed, 0)

    def take_mixed(i, c):
        b = lax.rem(chip + CHIPS - i, CHIPS) * 2 + 1 - core
        rcopy(mixed.at[b], mixed.at[b], sem.at[11], local_sem.at[b], (n, l)).wait_recv()
        return c

    lax.fori_loop(0, CHIPS, take_mixed, 0)
    seven = pl.ds(0, CHIPS - 1)
    rcopy(mixed.at[seven], mixed.at[seven], sem.at[11], local_sem.at[0], (n, l)).wait_send()
    eight = pl.ds(0, CHIPS)
    rcopy(mixed.at[eight], mixed.at[eight], sem.at[12], local_sem.at[0], (n, l)).wait_send()

    weights[2].wait()
    weights[3].wait()

    def expand(i, c):
        q = lax.rem(n // 2 + i, 4)
        wide = mixed[pl.ds(4 * q, 4)].reshape(192, COLS).astype(F32)
        scaled = (wide * gain[...]).astype(BF16)
        square = wide * wide
        lanes = square[:, :128]
        for t in range(1, COLS // 128):
            lanes += square[:, t * 128 : t * 128 + 128]
        gate = dot(scaled, wg[...]).astype(BF16)
        up = dot(scaled, wu[...]).astype(BF16)
        for k in range(2):
            to = 2 * q + k
            gu_send[to, :, :HID] = gate[k * NODE_ROWS : (k + 1) * NODE_ROWS]
            gu_send[to, :, HID:] = up[k * NODE_ROWS : (k + 1) * NODE_ROWS]
            sq_send[to] = jnp.zeros((8, 128), F32)
            sq_send[to, :, :NODE_ROWS] = lax.dot_general(
                jnp.ones((8, 128), F32),
                lanes[k * NODE_ROWS : (k + 1) * NODE_ROWS],
                NT,
                precision=lax.Precision.HIGHEST,
                preferred_element_type=F32,
            )

            @pl.when(to != n)
            def _():
                rcopy(gu_send.at[to], gu_recv.at[n], sem.at[13], sem.at[14], (to, l)).start()
                rcopy(sq_send.at[to], sq_recv.at[n], sem.at[15], sem.at[16], (to, l)).start()

        return c

    lax.fori_loop(1, 5, expand, 0)
    gu_recv[n] = gu_send[n]
    sq_recv[n] = sq_send[n]
    rcopy(sq_send.at[sent], sq_recv.at[sent], sem.at[15], sem.at[16], (n, l)).wait()
    mean = jnp.sum(sq_recv[...], axis=0) / D + EPS
    inverse = jnp.broadcast_to(lax.rsqrt(mean)[:1], (NODE_ROWS, 128))
    diagonal = lax.broadcasted_iota(jnp.int32, (NODE_ROWS, 128), 0) == lax.broadcasted_iota(
        jnp.int32, (NODE_ROWS, 128), 1
    )
    inverse = jnp.sum(jnp.where(diagonal, inverse, 0.0), axis=1, keepdims=True)
    rcopy(gu_send.at[sent], gu_recv.at[sent], sem.at[13], sem.at[14], (n, l)).wait()

    def activate(t, c):
        at = pl.multiple_of(t * 128, 128)
        gate = gu_recv[0, :, pl.ds(at, 128)].astype(F32)
        up = gu_recv[0, :, pl.ds(at + HID, 128)].astype(F32)
        for k in range(1, NODES):
            gate += gu_recv[k, :, pl.ds(at, 128)].astype(F32)
            up += gu_recv[k, :, pl.ds(at + HID, 128)].astype(F32)
        gate *= inverse
        up *= inverse
        hidden[n, :, pl.ds(at, 128)] = (gate / (1.0 + jnp.exp(-gate)) * up).astype(BF16)
        return c

    lax.fori_loop(0, HID // 128, activate, 0)

    def send_hidden(i, c):
        p = lax.rem(n + i, NODES)
        rcopy(hidden.at[n], hidden.at[n], sem.at[17], hid_sem.at[n], (p, l)).start()
        return c

    lax.fori_loop(1, NODES, send_hidden, 0)
    weights[4].wait()

    def take_hidden(i, c):
        p = lax.rem(n + NODES - i, NODES)
        rcopy(hidden.at[p], hidden.at[p], sem.at[17], hid_sem.at[p], (n, l)).wait_recv()
        return c

    lax.fori_loop(1, NODES, take_hidden, 0)
    rcopy(hidden.at[sent], hidden.at[sent], sem.at[17], hid_sem.at[0], (n, l)).wait_send()

    def down(q):
        return dot(hidden[pl.ds(2 * q, 2)].reshape(192, HID), wd[...])

    block_out = scatter(
        down, part2, pair2, pair_sem2, share_send2, share_recv2, sem.at[pl.ds(18, 2)], sem.at[20]
    )
    out[...] = (mixed[l].astype(F32) + block_out).astype(BF16)


def local(
    cache_pool, block_table, lengths, mig_slot, mig_dest, queries, new_entries, residual,
    w_uv, w_out, norm_gain, w_gate, w_up, w_down,
):
    n, l = lax.axis_index("node"), lax.axis_index("local")
    me = n * LOCALS + l
    leave = mig_slot[me]
    stay = 1 - leave
    own = lax.dynamic_slice_in_dim(lengths, me * 2, 2)
    ints = jnp.concatenate(
        [block_table[stay], block_table[leave], own[stay][None], own[leave][None], mig_dest]
    )
    by_slot = queries.reshape(STEPS, 2, HEADS, WIDTH)
    query_stay = lax.dynamic_index_in_dim(by_slot, stay, 1, keepdims=False).reshape(-1, WIDTH)
    leaving = lax.dynamic_index_in_dim(by_slot, leave, 1, keepdims=False)
    leaving = jnp.pad(leaving, ((0, 0), (0, 0), (0, 640 - WIDTH)))
    leaving = leaving.reshape(STEPS, HEADS // 16, 16, 5, 128).transpose(0, 1, 3, 2, 4).reshape(-1, 16, 128)
    fresh_stay = jnp.pad(lax.dynamic_index_in_dim(new_entries, stay, 1, keepdims=False), ((0, 13), (0, 0)))
    fresh_leave = lax.dynamic_index_in_dim(new_entries, leave, 1, keepdims=False)
    fresh_leave = jnp.pad(fresh_leave, ((0, 13), (0, 640 - WIDTH)))
    fresh_leave = fresh_leave.reshape(16, 5, 128).transpose(1, 0, 2)
    tiles = jnp.concatenate([leaving, fresh_leave, jnp.zeros((3, 16, 128), BF16)])
    device = jnp.arange(DEVS, dtype=jnp.int32)
    anchor = jnp.argmax(mig_dest[None, :] == device[:, None], axis=1).astype(jnp.int32)
    slot = jnp.arange(2, dtype=jnp.int32)
    request = jnp.where(slot[None, :] == mig_slot[:, None], anchor[:, None] * 2 + 1, device[:, None] * 2)
    source = request[:, :, None] * STEPS + jnp.arange(STEPS, dtype=jnp.int32)
    source = source.reshape(DEVS * 2 * STEPS, 1)
    resid = lax.dynamic_slice_in_dim(residual, l * 16, 16, 1).transpose(1, 0, 2).reshape(SHARE, COLS)

    vm = pl.BlockSpec(memory_space=pltpu.VMEM)
    hbm = pl.BlockSpec(memory_space=pl.ANY)
    dma = pltpu.SemaphoreType.DMA
    V = pltpu.VMEM
    result = pl.pallas_call(
        kernel,
        out_shape=jax.ShapeDtypeStruct((SHARE, COLS), BF16),
        in_specs=[pl.BlockSpec(memory_space=pltpu.SMEM)] + [vm] * 7 + [hbm] * 5,
        out_specs=vm,
        scratch_shapes=[
            V((8, LATENT, 128), BF16), V((1024, COLS), BF16), V((COLS, HID), BF16), V((COLS, HID), BF16),
            V((HID, COLS), BF16),
            V((DEVS, 16, 128), BF16), V((DEVS, 16, 128), BF16), V((DEVS, 16, 128), BF16),
            V((STEPS * HEADS, 640), BF16), V((16, 640), BF16),
            V((2, STEPS * HEADS, LATENT), F32),
            V((LOCALS, SHARE, LATENT), BF16), V((LOCALS, SHARE, LATENT), BF16),
            V((LATENT // 128, LOCALS * SHARE, 128), F32),
            V((NODES, NODE_ROWS, 1024), BF16), V((NODES, NODE_ROWS, COLS), BF16),
            V((2, CHIPS, SHARE, COLS), BF16), V((CHIPS, SHARE, COLS), BF16),
            V((CHIPS, SHARE, COLS), BF16), V((CHIPS, SHARE, COLS), BF16),
            V((LOCALS, SHARE, COLS), BF16),
            V((NODES, NODE_ROWS, 2 * HID), BF16), V((NODES, NODE_ROWS, 2 * HID), BF16),
            V((NODES, 8, 128), F32), V((NODES, 8, 128), F32),
            V((NODES, NODE_ROWS, HID), BF16),
            V((2, CHIPS, SHARE, COLS), BF16), V((CHIPS, SHARE, COLS), BF16),
            V((CHIPS, SHARE, COLS), BF16), V((CHIPS, SHARE, COLS), BF16),
            dma((5,)), pltpu.SemaphoreType.REGULAR, dma((21,)), dma((NODES,)), dma((LOCALS,)),
            dma((NODES,)), dma((4,)), dma((4,)),
        ],
        compiler_params=pltpu.CompilerParams(
            collective_id=0, has_side_effects=True, vmem_limit_bytes=60 * 2**20
        ),
        name="layer",
    )(
        ints, tiles, query_stay, fresh_stay, cache_pool, source, resid, norm_gain.reshape(1, COLS),
        w_uv, w_out, w_gate, w_up, w_down,
    )
    return result.reshape(16, STEPS, COLS).transpose(1, 0, 2)


def solution(mesh):
    in_specs = (
        P(("node", "local"), None, None),
        P(("node", "local"), None),
        P(),
        P(),
        P(),
        P(None, ("node", "local"), None),
        P(None, ("node", "local"), None),
        P(None, None, "node"),
        P("local", None, None),
        P("local", "node"),
        P("node"),
        P("node", "local"),
        P("node", "local"),
        P("local", "node"),
    )
    out_specs = P(None, "local", "node")
    return jax.shard_map(local, mesh=mesh, in_specs=in_specs, out_specs=out_specs, check_vma=False)
```

```python
import jax
import jax.numpy as jnp
from jax import lax
from jax.experimental import pallas as pl
from jax.experimental.pallas import tpu as pltpu
from jax.sharding import PartitionSpec as P

MESH = pl.DeviceIdType.MESH
BF16, F32 = jnp.bfloat16, jnp.float32
D = 7168
QK_NOPE = 128
LATENT = 512
ROPE = 64
WIDTH = LATENT + ROPE
STEPS = 3
HEADS = 128
NODES, LOCALS = 8, 16
DEVS = NODES * LOCALS
EPS = 1e-06
SCALE = (QK_NOPE + ROPE) ** (-0.5)
ROWS = 48
BATCH = NODES * ROWS
COLS = 896
HALF = 512
OFFSET = COLS - HALF
HID = 1152
KEYS = 640
NT = (((1,), (1,)), ((), ()))


def dot(a, b):
    return jnp.dot(a, b, preferred_element_type=F32)


def dot_nt(a, b):
    return lax.dot_general(a, b, NT, preferred_element_type=F32)


def iota(shape, dim):
    return lax.broadcasted_iota(jnp.int32, shape, dim)


def rcopy(src, dst, send, recv, device):
    return pltpu.make_async_remote_copy(
        src_ref=src, dst_ref=dst, send_sem=send, recv_sem=recv, device_id=device, device_id_type=MESH
    )


def attend(query, fresh, key0, key1, length):
    s0 = dot(query, key0) * SCALE
    s1 = dot(query, key1) * SCALE
    sf = dot_nt(query, fresh) * SCALE
    rows, block = s0.shape
    column = iota((rows, block), 1)
    s0 = jnp.where(column < length, s0, -jnp.inf)
    s1 = jnp.where(column + block < length, s1, -jnp.inf)
    step = iota(sf.shape, 0) // HEADS
    sf = jnp.where(iota(sf.shape, 1) <= step, sf, -jnp.inf)
    top = jnp.maximum(
        jnp.max(jnp.maximum(s0, s1), axis=1, keepdims=True), jnp.max(sf, axis=1, keepdims=True)
    )
    w0 = jnp.exp(s0 - top)
    w1 = jnp.exp(s1 - top)
    wf = jnp.exp(sf - top)
    total = jnp.sum(w0 + w1, axis=1, keepdims=True) + jnp.sum(wf, axis=1, keepdims=True)
    context = dot_nt(w0.astype(BF16), key0[:LATENT])
    context += dot_nt(w1.astype(BF16), key1[:LATENT])
    context += dot(wf.astype(BF16), fresh[:, :LATENT])
    return context / total


class Group:
    def __init__(self, pair, ring, block, device):
        self.p, self.r = pair, ring
        self.q = 1 - pair
        self.up, self.dn, self.op = lax.rem(ring + 1, 4), lax.rem(ring + 3, 4), lax.rem(ring + 2, 4)
        self.block, self.device = block, device


class Sems:
    def __init__(self, ref):
        self.ref, self.used, self.sent = ref, 0, []

    def take(self, count):
        first = self.used
        self.used += count
        return [self.ref.at[first + i] for i in range(count)]

    def start(self, src, dst, recv, device):
        copy = rcopy(src, dst, self.take(1)[0], recv, device)
        copy.start()
        self.sent.append(copy)


def arrived(ref, recv, here):
    rcopy(ref, ref, recv, recv, here).wait_recv()


def gather8(buf, g, sems, here, seen=None):
    width = buf.shape[-1] // 256 * 128
    lo, hi = pl.ds(0, width), pl.ds(width, buf.shape[-1] - width)
    recv = sems.take(8)
    b = g.block
    seen = seen or (lambda block: None)

    def send(block, to, index, cols=None):
        ref = buf.at[block] if cols is None else buf.at[block, :, cols]
        sems.start(ref, ref, recv[index], g.device(*to))

    def take(block, index, cols=None):
        arrived(buf.at[block] if cols is None else buf.at[block, :, cols], recv[index], here)

    own = b(g.p, g.r)
    send(own, (g.p, g.up), 2)
    send(own, (g.p, g.dn), 1)
    send(own, (g.q, g.r), 0)
    seen(own)
    yield
    take(b(g.p, g.up), 1)
    send(b(g.p, g.up), (g.p, g.dn), 5, lo)
    seen(b(g.p, g.up))
    take(b(g.p, g.dn), 2)
    send(b(g.p, g.dn), (g.p, g.up), 6, hi)
    seen(b(g.p, g.dn))
    take(b(g.q, g.r), 0)
    send(b(g.q, g.r), (g.p, g.up), 4)
    send(b(g.q, g.r), (g.p, g.dn), 3)
    seen(b(g.q, g.r))
    yield
    take(b(g.p, g.op), 5, lo)
    take(b(g.p, g.op), 6, hi)
    send(b(g.p, g.op), (g.q, g.r), 7)
    seen(b(g.p, g.op))
    yield
    take(b(g.q, g.up), 3)
    seen(b(g.q, g.up))
    take(b(g.q, g.dn), 4)
    seen(b(g.q, g.dn))
    take(b(g.q, g.op), 7)
    seen(b(g.q, g.op))


def scatter8(part, g, sems, here, own_plane, ra, rb, rc, rd, re, sc, sd, se):
    width = part.shape[-1] // 2
    halves = (pl.ds(0, width), pl.ds(width, width))
    recv = sems.take(10)
    b = g.block

    def wide(ref, *at):
        return ref[at].astype(F32)

    sems.start(part.at[b(g.q, g.op)], ra, recv[0], g.device(g.q, g.r))
    sems.start(part.at[b(g.q, g.up)], rb.at[0], recv[1], g.device(g.p, g.up))
    sems.start(part.at[b(g.q, g.dn)], rb.at[1], recv[2], g.device(g.p, g.dn))
    own_plane()
    up, dn = b(g.p, g.up), b(g.p, g.dn)
    sems.start(part.at[up, :, halves[1]], re.at[0, :, halves[1]], recv[6], g.device(g.p, g.up))
    sems.start(part.at[dn, :, halves[0]], re.at[1, :, halves[0]], recv[7], g.device(g.p, g.dn))
    yield
    arrived(ra, recv[0], here)
    sc[...] = (wide(part, b(g.p, g.op)) + wide(ra, ...)).astype(BF16)
    sems.start(sc.at[:, halves[0]], rc.at[0], recv[3], g.device(g.p, g.up))
    sems.start(sc.at[:, halves[1]], rc.at[1], recv[4], g.device(g.p, g.dn))
    arrived(rb.at[0], recv[1], here)
    arrived(rb.at[1], recv[2], here)
    sd[...] = (wide(part, b(g.q, g.r)) + wide(rb, 0) + wide(rb, 1)).astype(BF16)
    sems.start(sd, rd, recv[5], g.device(g.q, g.r))
    yield
    arrived(rc.at[0], recv[3], here)
    se[0] = (wide(part, up, slice(None), halves[0]) + wide(rc, 0)).astype(BF16)
    sems.start(se.at[0], re.at[0, :, halves[0]], recv[8], g.device(g.p, g.up))
    arrived(rc.at[1], recv[4], here)
    se[1] = (wide(part, dn, slice(None), halves[1]) + wide(rc, 1)).astype(BF16)
    sems.start(se.at[1], re.at[1, :, halves[1]], recv[9], g.device(g.p, g.dn))
    yield
    arrived(rd, recv[5], here)
    arrived(re.at[0, :, halves[1]], recv[6], here)
    arrived(re.at[1, :, halves[0]], recv[7], here)
    arrived(re.at[0, :, halves[0]], recv[8], here)
    arrived(re.at[1, :, halves[1]], recv[9], here)


def scatter8_shapes(cols):
    V = pltpu.VMEM
    return [
        V((2, ROWS, cols), BF16), V((2, 2, ROWS, cols), BF16), V((2, 2, ROWS, cols // 2), BF16),
        V((2, ROWS, cols), BF16), V((2, 2, ROWS, cols), BF16), V((2, ROWS, cols), BF16),
        V((2, ROWS, cols), BF16), V((2, 2, ROWS, cols // 2), BF16),
    ]


def kernel(
    table, lengths, slot_s, dest_s, slot_v, dest_v, gain, fresh_all,
    query_hbm, pool_hbm, resid_hbm, wuv_hbm, wout_hbm, wg_hbm, wu_hbm, wd_hbm,
    out, *scratch,
):
    refs = list(scratch)
    take = lambda count=1: [refs.pop(0) for _ in range(count)]
    query, pool, resid, wuv, wout, wg, wu, wd = take(8)
    tiles, r1, s2, r2, query_arr, fresh = take(6)
    ctx, ctx_send, ctx_recv, wide = take(4)
    values, part, pair, summed, mixed = take(5)
    attn_bufs = take(8)
    gu, sq_send, sq_recv, hidden = take(4)
    gu_bufs = take(8)
    part2, pair2, summed2, last, done = take(5)
    down_bufs = take(8)
    wsem, ready, far, ref_a, ref_b = take(5)

    n, l = lax.axis_index("node"), lax.axis_index("local")
    me = n * LOCALS + l
    here = (n, l)
    core, chip = lax.rem(l, 2), l // 2
    sibling = (n, l + 1 - 2 * core)
    mine = pl.multiple_of(core * OFFSET, 128)
    theirs = pl.multiple_of((1 - core) * OFFSET, 128)
    node = Group(n // 4, lax.rem(n, 4), lambda p, r: p * 4 + r, lambda p, r: (p * 4 + r, l))
    chips = Group(
        lax.rem(chip, 2), chip // 2, lambda p, r: r * 2 + p, lambda p, r: (n, (r * 2 + p) * 2 + core)
    )

    barrier = pltpu.get_barrier_semaphore()

    def greet_node(i, c):
        pl.semaphore_signal(barrier, inc=1, device_id=(lax.rem(n + i, NODES), l), device_id_type=MESH)
        return c

    def greet_local(i, c):
        pl.semaphore_signal(barrier, inc=1, device_id=(n, lax.rem(l + i, LOCALS)), device_id_type=MESH)
        return c

    def greet_all(i, c):
        pl.semaphore_signal(ready, inc=1, device_id=(n, lax.rem(l + i, LOCALS)), device_id_type=MESH)
        return c

    lax.fori_loop(1, NODES, greet_node, 0)
    lax.fori_loop(1, LOCALS, greet_local, 0)

    loads = [
        pltpu.make_async_copy(a, b, wsem.at[i])
        for i, (a, b) in enumerate(
            (
                (query_hbm, query), (pool_hbm, pool), (wuv_hbm, wuv), (wout_hbm, wout),
                (resid_hbm.at[:, pl.ds(chip * 32, 32), :], resid),
                (wg_hbm, wg), (wu_hbm, wu), (wd_hbm, wd),
            )
        )
    ]
    for copy in loads:
        copy.start()

    leave = slot_s[me]
    stay = 1 - leave

    fresh[...] = jnp.zeros(fresh.shape, BF16)
    both_fresh = fresh_all[...].astype(F32)
    fresh[0, :STEPS, :WIDTH] = jnp.where(stay == 0, both_fresh[:, 0], both_fresh[:, 1]).astype(BF16)
    fresh[1, :STEPS, :WIDTH] = jnp.where(stay == 1, both_fresh[:, 0], both_fresh[:, 1]).astype(BF16)
    loads[0].wait()
    blocks = HEADS // 16
    for s in range(STEPS):
        for hb in range(blocks):
            for cb in range(5):
                width = min(128, WIDTH - cb * 128)
                tiles[(s * blocks + hb) * 5 + cb, :, :width] = query[
                    s * 2 + leave, hb * 16 : hb * 16 + 16, cb * 128 : cb * 128 + width
                ]
    for cb in range(5):
        tiles[STEPS * blocks * 5 + cb] = fresh[1, :, cb * 128 : cb * 128 + 128]

    pl.semaphore_wait(barrier, NODES - 1 + LOCALS - 1)
    lax.fori_loop(1, LOCALS, greet_all, 0)
    pl.semaphore_wait(ready, LOCALS - 1)

    def spread(i, c):
        p = lax.rem(me + i, DEVS)
        rcopy(tiles.at[p], r1.at[me], far.at[0], far.at[1], (p // LOCALS, lax.rem(p, LOCALS))).start()
        return c

    lax.fori_loop(1, DEVS, spread, 0)
    r1[me] = tiles[me]
    loads[1].wait()

    def attention(j):
        if j == 0:
            request, new = stay, fresh[0, :, :WIDTH]
            rows = jnp.concatenate([query[s * 2 + stay] for s in range(STEPS)], axis=0)
        else:
            request, new = leave, fresh[1, :, :WIDTH]
            rows = query_arr[:, :WIDTH]
        key0, key1 = pool[table[request, 0]], pool[table[request, 1]]
        ctx[j] = attend(rows, new, key0, key1, lengths[me * 2 + request])

    others = pl.ds(0, LOCALS - 1)

    def send_context(j, sems):
        def group(g):
            at = pl.multiple_of(g * 8, 8)
            rows = jnp.concatenate([ctx[j, pl.ds(s * HEADS + at, 8), :] for s in range(STEPS)], axis=0)
            return jnp.concatenate([rows[:, :256], rows[:, 256:]], axis=0).astype(BF16)

        send, recv = sems.take(2)

        def send_group(i, c):
            g = lax.rem(l + i, LOCALS)
            ctx_send[j, g] = group(g)
            rcopy(ctx_send.at[j, g], ctx_recv.at[j, l], send, recv, (n, g)).start()
            return c

        lax.fori_loop(1, LOCALS, send_group, 0)
        ctx_recv[j, l] = group(l)
        return rcopy(ctx_send.at[j, others], ctx_recv.at[j, others], send, recv, here)

    def select(rows, columns, test):
        return jnp.where(test(iota((rows, columns), 0), iota((rows, columns), 1)), 1.0, 0.0).astype(BF16)

    def slots(rows, device):
        lanes = jnp.broadcast_to(slot_v[...], (rows, DEVS)).astype(F32)
        at = device(iota((rows, DEVS), 0)) == iota((rows, DEVS), 1)
        return jnp.sum(jnp.where(at, lanes, 0.0), axis=1, keepdims=True).astype(jnp.int32)

    def halves(product, part, pair, summed, j, sems):
        part[j] = product.reshape(NODES, ROWS, COLS)
        recv = sems.take(1)[0]
        sems.start(part.at[j, :, :, pl.ds(theirs, HALF)], pair.at[j], recv, sibling)
        yield
        arrived(pair.at[j], recv, here)
        summed[j] = (part[j, :, :, pl.ds(mine, HALF)].astype(F32) + pair[j].astype(F32)).astype(BF16)

    def total(bufs, part, g, j):
        own = part[j, g.block(g.p, g.r)].astype(F32)
        rd, re = bufs[3], bufs[4]
        return own + rd[j].astype(F32) + re[j, 0].astype(F32) + re[j, 1].astype(F32)

    def chain(j, sems, context):
        if j == 0:
            loads[2].wait()
        context.wait()
        for t in range(2):
            got = ctx_recv[j, :, :, t * 128 : t * 128 + 128].astype(F32)
            for half in range(2):
                for s in range(STEPS):
                    at = half * 24 + s * 8
                    wide[half * 2 + t, s * 128 : s * 128 + 128] = got[:, at : at + 8].reshape(128, 128)
        for h in range(8):
            rows = [wide[t, pl.ds(h, ROWS, stride=8), :] for t in range(LATENT // 128)]
            rows = jnp.concatenate(rows, axis=1).astype(BF16)
            values[j, n, :, h * 128 : h * 128 + 128] = dot(rows, wuv[h]).astype(BF16)
        yield from gather8(values.at[j], node, sems, here)
        if j == 0:
            loads[3].wait()
        product = dot(values[j].reshape(BATCH, 1024), wout[...]).astype(BF16)
        if j == 1:
            pick = select(DEVS, DEVS, lambda row, column: dest_v[...] == row)
            by_step = product.reshape(NODES, STEPS, LOCALS, COLS)
            moved = [dot(pick, by_step[:, s].reshape(DEVS, COLS)).astype(BF16) for s in range(STEPS)]
            moved = [m.reshape(NODES, LOCALS, COLS) for m in moved]
            product = jnp.concatenate(moved, axis=1)
        yield from halves(product, part, pair, summed, j, sems)
        yield from scatter8(
            summed.at[j], chips, sems, here, lambda: None, *[r.at[j] for r in attn_bufs]
        )
        if j == 0:
            loads[4].wait()
        slot = slots(LOCALS, lambda row: chip * LOCALS + row)
        pick = select(
            LOCALS, 2 * LOCALS,
            lambda row, column: (column // 2 == row) & ((lax.rem(column, 2) == slot) == (j == 1)),
        )
        skip = [dot(pick, resid[s, :, pl.ds(mine, HALF)]) for s in range(STEPS)]
        mixed[j, core, chip] = (jnp.concatenate(skip, axis=0) + total(attn_bufs, summed, chips, j)).astype(BF16)

        side = sems.take(8)
        side_ref = sems.ref.at[pl.ds(sems.used - 8, 8)]

        def on(block):
            ref = mixed.at[j, core, block]
            sems.start(ref, ref, side_ref.at[block], sibling)

        yield from gather8(mixed.at[j, core], chips, sems, here, on)
        for block in range(NODES):
            arrived(mixed.at[j, 1 - core, block], side[block], here)

        if j == 0:
            loads[5].wait()
            loads[6].wait()

        sq = sems.take(2)

        def expand(plane):
            at = pl.ds(plane * 4, 4)
            left = mixed[j, 0, at].reshape(4 * ROWS, HALF).astype(F32)
            right = mixed[j, 1, at, :, HALF - OFFSET :].reshape(4 * ROWS, OFFSET).astype(F32)
            rows = jnp.concatenate([left, right], axis=1)
            scaled = (rows * gain[...]).astype(BF16)
            square = rows * rows
            lanes = square[:, :128]
            for t in range(1, COLS // 128):
                lanes += square[:, t * 128 : t * 128 + 128]
            gu[j, at, :, :HID] = dot(scaled, wg[...]).astype(BF16).reshape(4, ROWS, HID)
            gu[j, at, :, HID:] = dot(scaled, wu[...]).astype(BF16).reshape(4, ROWS, HID)
            for k in range(4):
                to = plane * 4 + k
                sums = lax.dot_general(
                    jnp.ones((8, 128), F32), lanes[k * ROWS : (k + 1) * ROWS], NT,
                    precision=lax.Precision.HIGHEST, preferred_element_type=F32,
                )
                sq_send[j, to] = jnp.concatenate([sums, jnp.zeros((8, 128 - ROWS), F32)], axis=1)

        def own_plane():
            expand(node.p)

            def send_sq(i, c):
                p = lax.rem(n + i, NODES)
                rcopy(sq_send.at[j, p], sq_recv.at[j, n], sq[0], sq[1], (p, l)).start()
                return c

            lax.fori_loop(1, NODES, send_sq, 0)
            sq_recv[j, n] = sq_send[j, n]

        expand(node.q)
        yield from scatter8(gu.at[j], node, sems, here, own_plane, *[r.at[j] for r in gu_bufs])
        seven = pl.ds(0, NODES - 1)
        rcopy(sq_send.at[j, seven], sq_recv.at[j, seven], sq[0], sq[1], here).wait()
        inverse = lax.rsqrt(jnp.sum(sq_recv[j], axis=0) / D + EPS)
        inverse = jnp.broadcast_to(inverse[:1], (ROWS, 128))
        inverse = jnp.where(iota((ROWS, 128), 0) == iota((ROWS, 128), 1), inverse, 0.0)
        inverse = jnp.sum(inverse, axis=1, keepdims=True)
        summed_gu = total(gu_bufs, gu, node, j) * inverse
        gate, up = summed_gu[:, :HID], summed_gu[:, HID:]
        hidden[j, n] = (gate / (1.0 + jnp.exp(-gate)) * up).astype(BF16)
        yield from gather8(hidden.at[j], node, sems, here)
        if j == 0:
            loads[7].wait()
        product = dot(hidden[j].reshape(BATCH, HID), wd[...]).astype(BF16)
        yield from halves(product, part2, pair2, summed2, j, sems)
        yield from scatter8(
            summed2.at[j], chips, sems, here, lambda: None, *[r.at[j] for r in down_bufs]
        )
        last[j, core] = (mixed[j, core, chip].astype(F32) + total(down_bufs, summed2, chips, j)).astype(BF16)
        recv = sems.take(1)[0]
        sems.start(last.at[j, core], last.at[j, core], recv, sibling)
        yield
        arrived(last.at[j, 1 - core], recv, here)

    sems = [Sems(ref_a), Sems(ref_b)]
    attention(0)
    context = send_context(0, sems[0])

    both = pl.ds(0, DEVS - 1)
    rcopy(tiles.at[both], r1.at[both], far.at[0], far.at[1], here).wait()

    def sort(o, c):
        s2[o] = r1[dest_s[o]]
        return c

    lax.fori_loop(0, DEVS, sort, 0)

    def deliver(i, c):
        p = lax.rem(me + i, DEVS)
        rcopy(s2.at[p], r2.at[me], far.at[2], far.at[3], (p // LOCALS, lax.rem(p, LOCALS))).start()
        return c

    lax.fori_loop(1, DEVS, deliver, 0)
    r2[me] = s2[me]

    first = chain(0, sems[0], context)
    for _ in range(LEAD):
        next(first)
    rcopy(s2.at[both], r2.at[both], far.at[2], far.at[3], here).wait()
    for s in range(STEPS):
        for hb in range(blocks):
            for cb in range(5):
                query_arr[s * HEADS + hb * 16 : s * HEADS + hb * 16 + 16, cb * 128 : cb * 128 + 128] = r2[
                    (s * blocks + hb) * 5 + cb
                ]
    for cb in range(5):
        fresh[1, :, cb * 128 : cb * 128 + 128] = r2[STEPS * blocks * 5 + cb]
    attention(1)
    context = send_context(1, sems[1])
    next(first, None)
    chains = [chain(1, sems[1], context), first]
    while chains:
        for steps in list(chains):
            try:
                next(steps)
            except StopIteration:
                chains.remove(steps)

    slot = slots(LOCALS, lambda row: chip * LOCALS + core * 8 + row // 2)
    pick = select(
        LOCALS, LOCALS,
        lambda row, column: (lax.rem(column, 8) == row // 2) & ((lax.rem(row, 2) == slot) == (column >= 8)),
    )
    at = pl.multiple_of(core * 8, 8)
    for j in range(2):
        done[j, :, :HALF] = last[j, 0].astype(F32)
        done[j, :, HALF:] = last[j, 1, :, HALF - OFFSET :].astype(F32)
    for s in range(STEPS):
        rows = jnp.concatenate([done[j, pl.ds(s * LOCALS + at, 8), :] for j in range(2)], axis=0).astype(BF16)
        out[s] = dot(pick, rows).astype(BF16)
    for one in sems:
        for copy in one.sent:
            copy.wait_send()


LEAD = 2


def local(
    cache_pool, block_table, lengths, mig_slot, mig_dest, queries, new_entries, residual,
    w_uv, w_out, norm_gain, w_gate, w_up, w_down,
):
    by_slot = queries.reshape(STEPS * 2, HEADS, WIDTH)
    vm = pl.BlockSpec(memory_space=pltpu.VMEM)
    hbm = pl.BlockSpec(memory_space=pl.ANY)
    smem = pl.BlockSpec(memory_space=pltpu.SMEM)
    dma = pltpu.SemaphoreType.DMA
    V = pltpu.VMEM
    tile = (DEVS, 16, 128)
    return pl.pallas_call(
        kernel,
        out_shape=jax.ShapeDtypeStruct((STEPS, LOCALS, COLS), BF16),
        in_specs=[smem] * 4 + [vm] * 4 + [hbm] * 8,
        out_specs=vm,
        scratch_shapes=[
            V((STEPS * 2, HEADS, WIDTH), BF16), V((4, WIDTH, 256), BF16), V((STEPS, 32, COLS), BF16),
            V((8, LATENT, 128), BF16), V((1024, COLS), BF16), V((COLS, HID), BF16), V((COLS, HID), BF16),
            V((HID, COLS), BF16),
            V(tile, BF16), V(tile, BF16), V(tile, BF16), V(tile, BF16),
            V((STEPS * HEADS, KEYS), BF16), V((2, 16, KEYS), BF16),
            V((2, STEPS * HEADS, LATENT), F32),
            V((2, LOCALS, ROWS, 256), BF16), V((2, LOCALS, ROWS, 256), BF16),
            V((LATENT // 128, BATCH, 128), F32),
            V((2, NODES, ROWS, 1024), BF16), V((2, NODES, ROWS, COLS), BF16),
            V((2, NODES, ROWS, HALF), BF16), V((2, NODES, ROWS, HALF), BF16),
            V((2, 2, NODES, ROWS, HALF), BF16),
            *scatter8_shapes(HALF),
            V((2, NODES, ROWS, 2 * HID), BF16), V((2, NODES, 8, 128), F32), V((2, NODES, 8, 128), F32),
            V((2, NODES, ROWS, HID), BF16),
            *scatter8_shapes(2 * HID),
            V((2, NODES, ROWS, COLS), BF16), V((2, NODES, ROWS, HALF), BF16), V((2, NODES, ROWS, HALF), BF16),
            V((2, 2, ROWS, HALF), BF16), V((2, ROWS, COLS), F32),
            *scatter8_shapes(HALF),
            dma((8,)), pltpu.SemaphoreType.REGULAR, dma((4,)), dma((160,)), dma((160,)),
        ],
        compiler_params=pltpu.CompilerParams(
            collective_id=0, has_side_effects=True, vmem_limit_bytes=60 * 2**20
        ),
        name="layer",
    )(
        block_table, lengths, mig_slot, mig_dest, mig_slot.reshape(1, DEVS), mig_dest.reshape(1, DEVS),
        norm_gain.reshape(1, COLS), new_entries,
        by_slot, cache_pool, residual, w_uv, w_out, w_gate, w_up, w_down,
    )


def solution(mesh):
    in_specs = (
        P(("node", "local"), None, None),
        P(("node", "local"), None),
        P(),
        P(),
        P(),
        P(None, ("node", "local"), None),
        P(None, ("node", "local"), None),
        P(None, None, "node"),
        P("local", None, None),
        P("local", "node"),
        P("node"),
        P("node", "local"),
        P("node", "local"),
        P("local", "node"),
    )
    out_specs = P(None, "local", "node")
    return jax.shard_map(local, mesh=mesh, in_specs=in_specs, out_specs=out_specs, check_vma=False)
```

```python
import jax
import jax.numpy as jnp
from jax import lax
from jax.experimental import pallas as pl
from jax.experimental.pallas import tpu as pltpu
from jax.sharding import PartitionSpec as P

MESH = pl.DeviceIdType.MESH
BF16, F32 = jnp.bfloat16, jnp.float32
D = 7168
QK_NOPE = 128
LATENT = 512
ROPE = 64
WIDTH = LATENT + ROPE
STEPS = 3
HEADS = 128
NODES, LOCALS = 8, 16
DEVS = NODES * LOCALS
EPS = 1e-06
SCALE = (QK_NOPE + ROPE) ** (-0.5)
COLS = 896
HALF = 512
OFFSET = COLS - HALF
HID = 1152
KEYS = 640
NT = (((1,), (1,)), ((), ()))


def dot(a, b):
    return jnp.dot(a, b, preferred_element_type=F32)


def dot_nt(a, b):
    return lax.dot_general(a, b, NT, preferred_element_type=F32)


def iota(shape, dim):
    return lax.broadcasted_iota(jnp.int32, shape, dim)


def rcopy(src, dst, send, recv, device):
    return pltpu.make_async_remote_copy(
        src_ref=src, dst_ref=dst, send_sem=send, recv_sem=recv, device_id=device, device_id_type=MESH
    )


def attend(query, fresh, key0, key1, length):
    s0 = dot(query, key0) * SCALE
    s1 = dot(query, key1) * SCALE
    sf = dot_nt(query, fresh) * SCALE
    rows, block = s0.shape
    column = iota((rows, block), 1)
    s0 = jnp.where(column < length, s0, -jnp.inf)
    s1 = jnp.where(column + block < length, s1, -jnp.inf)
    step = iota(sf.shape, 0) // HEADS
    sf = jnp.where(iota(sf.shape, 1) <= step, sf, -jnp.inf)
    top = jnp.maximum(
        jnp.max(jnp.maximum(s0, s1), axis=1, keepdims=True), jnp.max(sf, axis=1, keepdims=True)
    )
    w0 = jnp.exp(s0 - top)
    w1 = jnp.exp(s1 - top)
    wf = jnp.exp(sf - top)
    total = jnp.sum(w0 + w1, axis=1, keepdims=True) + jnp.sum(wf, axis=1, keepdims=True)
    context = dot_nt(w0.astype(BF16), key0[:LATENT])
    context += dot_nt(w1.astype(BF16), key1[:LATENT])
    context += dot(wf.astype(BF16), fresh[:, :LATENT])
    return context / total


class Group:
    def __init__(self, pair, ring, block, device):
        self.p, self.r = pair, ring
        self.q = 1 - pair
        self.up, self.dn, self.op = lax.rem(ring + 1, 4), lax.rem(ring + 3, 4), lax.rem(ring + 2, 4)
        self.block, self.device = block, device


class Pool:
    def __init__(self, ref):
        self.ref, self.free, self.used = ref, [], 0

    def take(self):
        if self.free:
            return self.free.pop()
        self.used += 1
        return self.used - 1


class Sems:
    def __init__(self, ref, pool):
        self.ref, self.pool, self.used, self.sent, self.older = ref, pool, 0, [], []

    def take(self, count):
        first = self.used
        self.used += count
        return [self.ref.at[first + i] for i in range(count)]

    def sender(self):
        index = self.pool.take()
        return index, self.pool.ref.at[index]

    def keep(self, index, copy):
        self.sent.append((index, copy))

    def start(self, src, dst, recv, device):
        index, send = self.sender()
        copy = rcopy(src, dst, send, recv, device)
        copy.start()
        self.keep(index, copy)

    def settle(self):
        for index, copy in self.older:
            copy.wait_send()
            self.pool.free.append(index)
        self.older, self.sent = self.sent, []


def arrived(ref, recv, here):
    rcopy(ref, ref, recv, recv, here).wait_recv()


def gather8(buf, g, sems, here):
    width = buf.shape[-1] // 256 * 128
    lo, hi = pl.ds(0, width), pl.ds(width, buf.shape[-1] - width)
    recv = sems.take(5)
    b = g.block

    def send(block, to, index, cols=None):
        ref = buf.at[block] if cols is None else buf.at[block, :, cols]
        sems.start(ref, ref, recv[index], g.device(*to))

    own = b(g.p, g.r)
    send(own, (g.p, g.up), 1)
    send(own, (g.p, g.dn), 0)
    send(own, (g.q, g.r), 2)
    yield
    arrived(buf.at[b(g.p, g.up)], recv[0], here)
    send(b(g.p, g.up), (g.p, g.dn), 3, lo)
    arrived(buf.at[b(g.p, g.dn)], recv[1], here)
    send(b(g.p, g.dn), (g.p, g.up), 3, hi)
    arrived(buf.at[b(g.q, g.r)], recv[2], here)
    send(b(g.q, g.r), (g.p, g.up), 4)
    send(b(g.q, g.r), (g.p, g.dn), 4)
    yield
    arrived(buf.at[b(g.p, g.op)], recv[3], here)
    send(b(g.p, g.op), (g.q, g.r), 4)
    yield
    arrived(buf.at[pl.ds(0, 3)], recv[4], here)


def scatter8(part, g, sems, here, meanwhile, ra, rb, rc, rd, re, sc, sd, se):
    width = part.shape[-1] // 2
    halves = (pl.ds(0, width), pl.ds(width, width))
    recv = sems.take(5)
    b = g.block

    def wide(ref, *at):
        return ref[at].astype(F32)

    sems.start(part.at[b(g.q, g.op)], ra, recv[0], g.device(g.q, g.r))
    sems.start(part.at[b(g.q, g.up)], rb.at[0], recv[1], g.device(g.p, g.up))
    sems.start(part.at[b(g.q, g.dn)], rb.at[1], recv[1], g.device(g.p, g.dn))
    meanwhile()
    up, dn = b(g.p, g.up), b(g.p, g.dn)
    yield
    arrived(ra, recv[0], here)
    sc[...] = (wide(part, b(g.p, g.op)) + wide(ra, ...)).astype(BF16)
    sems.start(sc.at[:, halves[0]], rc.at[0], recv[2], g.device(g.p, g.up))
    sems.start(sc.at[:, halves[1]], rc.at[1], recv[2], g.device(g.p, g.dn))
    sems.start(part.at[up, :, halves[1]], re.at[0, :, halves[1]], recv[4], g.device(g.p, g.up))
    sems.start(part.at[dn, :, halves[0]], re.at[1, :, halves[0]], recv[4], g.device(g.p, g.dn))
    arrived(rb, recv[1], here)
    sd[...] = (wide(part, b(g.q, g.r)) + wide(rb, 0) + wide(rb, 1)).astype(BF16)
    sems.start(sd, rd, recv[3], g.device(g.q, g.r))
    yield
    arrived(rc, recv[2], here)
    se[0] = (wide(part, up, slice(None), halves[0]) + wide(rc, 0)).astype(BF16)
    sems.start(se.at[0], re.at[0, :, halves[0]], recv[4], g.device(g.p, g.up))
    se[1] = (wide(part, dn, slice(None), halves[1]) + wide(rc, 1)).astype(BF16)
    sems.start(se.at[1], re.at[1, :, halves[1]], recv[4], g.device(g.p, g.dn))
    yield
    arrived(rd, recv[3], here)
    arrived(re, recv[4], here)


def ring_scatter(part, got, away, g, sems, here):
    recv = sems.take(1)[0]
    for i, ring in enumerate((g.up, g.dn, g.op)):
        sems.start(part.at[pl.ds(ring * 2, 2)], got.at[i], recv, g.device(g.p, ring))
    yield
    arrived(got, recv, here)
    terms = [part[pl.ds(g.r * 2, 2)]] + [got[i] for i in range(3)]
    away[...] = sum(t.astype(F32) for t in terms).astype(BF16)


def scatter1(part, got, own, device, sems, here):
    recv = sems.take(1)[0]
    index, send = sems.sender()

    def spread(i, c):
        to = lax.rem(own + i, 8)
        rcopy(part.at[to], got.at[own], send, recv, device(to)).start()
        return c

    lax.fori_loop(1, 8, spread, 0)
    got[own] = part[own]
    seven = pl.ds(0, 7)
    sems.keep(index, rcopy(part.at[seven], got.at[seven], send, recv, here))
    yield
    rcopy(part.at[seven], got.at[seven], send, recv, here).wait_recv()


def ring_shapes(rows, cols):
    V = pltpu.VMEM
    return [V((3, 2, rows, cols), BF16), V((2, rows, cols), BF16), V((2, rows, cols), BF16)]


def scatter8_shapes(rows, cols):
    V = pltpu.VMEM
    return [
        V((rows, cols), BF16), V((2, rows, cols), BF16), V((2, rows, cols // 2), BF16),
        V((rows, cols), BF16), V((2, rows, cols), BF16), V((rows, cols), BF16),
        V((rows, cols), BF16), V((2, rows, cols // 2), BF16),
    ]


def chain_shapes(steps):
    V = pltpu.VMEM
    rows = LOCALS * steps
    return [
        V((LOCALS, rows, 256), BF16), V((LOCALS, rows, 256), BF16), V((LATENT // 128, 8 * rows, 128), F32),
        V((NODES, rows, 1024), BF16), V((NODES, rows, COLS), BF16),
        V((NODES, rows, HALF), BF16), V((NODES, rows, HALF), BF16), V((2, NODES, rows, HALF), BF16),
        *ring_shapes(rows, HALF),
        V((NODES, rows, 2 * HID), BF16), V((8, NODES * rows), F32), V((NODES, 8, NODES * rows), F32),
        V((NODES, rows, HID), BF16),
        *scatter8_shapes(rows, 2 * HID),
        V((NODES, rows, COLS), BF16), V((NODES, rows, HALF), BF16), V((NODES, rows, HALF), BF16),
        V((NODES, rows, HALF), BF16), V((2, rows, HALF), BF16), V((rows, COLS), F32),
    ]


def kernel(
    table, lengths, slot_s, dest_s, slot_v, dest_v, gain, fresh_all,
    query_hbm, pool_hbm, resid_hbm, wuv_hbm, wout_hbm, wg_hbm, wu_hbm, wd_hbm,
    out, *scratch,
):
    refs = list(scratch)
    take = lambda count=1: [refs.pop(0) for _ in range(count)]
    query, pool, resid, wuv, wout, wg, wu, wd = take(8)
    tiles, r1, s2, r2, query_arr, fresh, ctx = take(7)
    bufs = [take(len(chain_shapes(1))) for _ in CHAINS]
    wsem, ready, far, senders = take(4)
    senders = Pool(senders)
    sems = [Sems(ref, senders) for ref in take(len(CHAINS))]

    n, l = lax.axis_index("node"), lax.axis_index("local")
    me = n * LOCALS + l
    here = (n, l)
    core, chip = lax.rem(l, 2), l // 2
    sibling = (n, l + 1 - 2 * core)
    mine = pl.multiple_of(core * OFFSET, 128)
    theirs = pl.multiple_of((1 - core) * OFFSET, 128)
    node = Group(n // 4, lax.rem(n, 4), lambda p, r: p * 4 + r, lambda p, r: (p * 4 + r, l))
    chips = Group(
        lax.rem(chip, 2), chip // 2, lambda p, r: r * 2 + p, lambda p, r: (n, (r * 2 + p) * 2 + core)
    )

    barrier = pltpu.get_barrier_semaphore()

    def greet_node(i, c):
        pl.semaphore_signal(barrier, inc=1, device_id=(lax.rem(n + i, NODES), l), device_id_type=MESH)
        return c

    def greet_local(i, c):
        pl.semaphore_signal(barrier, inc=1, device_id=(n, lax.rem(l + i, LOCALS)), device_id_type=MESH)
        return c

    def greet_all(i, c):
        pl.semaphore_signal(ready, inc=1, device_id=(n, lax.rem(l + i, LOCALS)), device_id_type=MESH)
        return c

    lax.fori_loop(1, NODES, greet_node, 0)
    lax.fori_loop(1, LOCALS, greet_local, 0)

    loads = [
        pltpu.make_async_copy(a, b, wsem.at[i])
        for i, (a, b) in enumerate(
            (
                (query_hbm, query), (pool_hbm, pool), (wuv_hbm, wuv), (wout_hbm, wout),
                (resid_hbm.at[:, pl.ds(chip // 2 * 64, 64), :], resid),
                (wg_hbm, wg), (wu_hbm, wu), (wd_hbm, wd),
            )
        )
    ]
    for copy in loads:
        copy.start()

    gain_row = gain[...].reshape(1, COLS)
    leave = slot_s[me]
    stay = 1 - leave

    fresh[...] = jnp.zeros(fresh.shape, BF16)
    both_fresh = fresh_all[...].astype(F32)
    fresh[0, :STEPS, :WIDTH] = jnp.where(stay == 0, both_fresh[:, 0], both_fresh[:, 1]).astype(BF16)
    fresh[1, :STEPS, :WIDTH] = jnp.where(stay == 1, both_fresh[:, 0], both_fresh[:, 1]).astype(BF16)
    loads[0].wait()
    blocks = HEADS // 16
    for s in range(STEPS):
        for hb in range(blocks):
            for cb in range(5):
                width = min(128, WIDTH - cb * 128)
                tiles[(s * blocks + hb) * 5 + cb, :, :width] = query[
                    s * 2 + leave, hb * 16 : hb * 16 + 16, cb * 128 : cb * 128 + width
                ]
    for cb in range(5):
        tiles[STEPS * blocks * 5 + cb] = fresh[1, :, cb * 128 : cb * 128 + 128]

    def spread(i, c):
        p = lax.rem(me + i, DEVS)
        rcopy(tiles.at[p], r1.at[me], far.at[0], far.at[1], (p // LOCALS, lax.rem(p, LOCALS))).start()
        return c

    r1[me] = tiles[me]

    def attention(j):
        if j == 0:
            request, new = stay, fresh[0, :, :WIDTH]
            rows = jnp.concatenate([query[s * 2 + stay] for s in range(STEPS)], axis=0)
        else:
            request, new = leave, fresh[1, :, :WIDTH]
            rows = query_arr[:, :WIDTH]
        key0, key1 = pool[table[request, 0]], pool[table[request, 1]]
        ctx[j] = attend(rows, new, key0, key1, lengths[me * 2 + request])

    others = pl.ds(0, LOCALS - 1)

    def send_context(j, steps, bufs, sems):
        ctx_send, ctx_recv = bufs[:2]

        def group(g):
            at = pl.multiple_of(g * 8, 8)
            rows = jnp.concatenate([ctx[j, pl.ds(s * HEADS + at, 8), :] for s in steps], axis=0)
            return jnp.concatenate([rows[:, :256], rows[:, 256:]], axis=0).astype(BF16)

        send, recv = sems.take(2)

        def send_group(i, c):
            g = lax.rem(l + i, LOCALS)
            ctx_send[g] = group(g)
            rcopy(ctx_send.at[g], ctx_recv.at[l], send, recv, (n, g)).start()
            return c

        lax.fori_loop(1, LOCALS, send_group, 0)
        ctx_recv[l] = group(l)
        return rcopy(ctx_send.at[others], ctx_recv.at[others], send, recv, here)

    def select(rows, columns, test):
        return jnp.where(test(iota((rows, columns), 0), iota((rows, columns), 1)), 1.0, 0.0).astype(BF16)

    def slots(rows, device):
        lanes = jnp.broadcast_to(slot_v[...], (rows, DEVS)).astype(F32)
        at = device(iota((rows, DEVS), 0)) == iota((rows, DEVS), 1)
        return jnp.sum(jnp.where(at, lanes, 0.0), axis=1, keepdims=True).astype(jnp.int32)

    def chain(j, steps, bufs, sems, context, only):
        count = len(steps)
        rows = LOCALS * count
        bufs = list(bufs)
        take = lambda count=1: [bufs.pop(0) for _ in range(count)]
        ctx_send, ctx_recv, wide, values, part, pair, summed, mixed = take(8)
        got, away, back = take(3)
        gu, sq_send, sq_recv, hidden = take(4)
        gu_bufs = take(8)
        part2, pair2, summed2 = take(3)
        got2 = take()[0]
        last, done = take(2)

        def halves(product, part, pair, summed):
            part[...] = product.reshape(NODES, rows, COLS)
            recv = sems.take(1)[0]
            sems.start(part.at[:, :, pl.ds(theirs, HALF)], pair, recv, sibling)
            yield
            arrived(pair, recv, here)
            summed[...] = (part[:, :, pl.ds(mine, HALF)].astype(F32) + pair[...].astype(F32)).astype(BF16)

        if only:
            loads[2].wait()
        context.wait()
        for t in range(2):
            recv = ctx_recv[:, :, t * 128 : t * 128 + 128].astype(F32)
            for half in range(2):
                for s in range(count):
                    at = (half * count + s) * 8
                    wide[half * 2 + t, s * 128 : s * 128 + 128] = recv[:, at : at + 8].reshape(128, 128)
        for h in range(8):
            head = [wide[t, pl.ds(h, rows, stride=8), :] for t in range(LATENT // 128)]
            head = jnp.concatenate(head, axis=1).astype(BF16)
            values[n, :, h * 128 : h * 128 + 128] = dot(head, wuv[h]).astype(BF16)
        yield from gather8(values, node, sems, here)
        if only:
            loads[3].wait()
        product = dot(values[...].reshape(NODES * rows, 1024), wout[...]).astype(BF16)
        if j == 1:
            pick = select(DEVS, DEVS, lambda row, column: dest_v[...] == row)
            by_step = product.reshape(NODES, count, LOCALS, COLS)
            moved = [dot(pick, by_step[:, s].reshape(DEVS, COLS)).astype(BF16) for s in range(count)]
            product = jnp.concatenate([m.reshape(NODES, LOCALS, COLS) for m in moved], axis=1)
        yield from halves(product, part, pair, summed)

        yield from ring_scatter(summed, got, away, chips, sems, here)
        recv = sems.take(1)[0]
        sems.start(away, back, recv, chips.device(chips.q, chips.r))
        if only:
            loads[4].wait()
        slot = slots(2 * LOCALS, lambda row: chips.r * 2 * LOCALS + row)
        pick = select(
            2 * LOCALS, 4 * LOCALS,
            lambda row, column: (column // 2 == row) & ((lax.rem(column, 2) == slot) == (j == 1)),
        )
        skip = [dot(pick, resid[s, :, pl.ds(mine, HALF)]) for s in steps]
        skip = jnp.concatenate([k.reshape(2, LOCALS, HALF) for k in skip], axis=1)
        yield
        arrived(back, recv, here)
        two = pl.ds(chips.r * 2, 2)
        mixed[core, two] = (skip + (away[...].astype(F32) + back[...].astype(F32))).astype(BF16)

        side = sems.take(1)[0]
        recv = sems.take(3)

        def pass_on(ring):
            ref = mixed.at[core, pl.ds(ring * 2, 2)]
            sems.start(ref, ref, side, sibling)

        for i, ring in enumerate((chips.up, chips.dn, chips.op)):
            ref = mixed.at[core, two]
            sems.start(ref, ref, recv[i], chips.device(chips.p, ring))
        pass_on(chips.r)
        yield
        for i, ring in enumerate((chips.dn, chips.up, chips.op)):
            arrived(mixed.at[core, pl.ds(ring * 2, 2)], recv[i], here)
            pass_on(ring)
        arrived(mixed.at[1 - core], side, here)

        if only:
            loads[5].wait()
            loads[6].wait()
        sq = sems.take(2)

        left = mixed[0].reshape(NODES * rows, HALF).astype(F32)
        right = mixed[1, :, :, HALF - OFFSET :].reshape(NODES * rows, OFFSET).astype(F32)
        whole = jnp.concatenate([left, right], axis=1)
        scaled = (whole * gain_row).astype(BF16)
        gu[:, :, :HID] = dot(scaled, wg[...]).astype(BF16).reshape(NODES, rows, HID)
        gu[:, :, HID:] = dot(scaled, wu[...]).astype(BF16).reshape(NODES, rows, HID)

        def squares():
            square = whole * whole
            lanes = square[:, :128]
            for t in range(1, COLS // 128):
                lanes += square[:, t * 128 : t * 128 + 128]
            sq_send[...] = lax.dot_general(
                jnp.ones((8, 128), F32), lanes, NT, precision=lax.Precision.HIGHEST, preferred_element_type=F32
            )

            def send_sq(i, c):
                p = lax.rem(n + i, NODES)
                rcopy(sq_send, sq_recv.at[n], sq[0], sq[1], (p, l)).start()
                return c

            lax.fori_loop(1, NODES, send_sq, 0)
            sq_recv[n] = sq_send[...]

        yield from scatter8(gu, node, sems, here, squares, *gu_bufs)
        seven = pl.ds(0, NODES - 1)
        rcopy(sq_recv.at[seven], sq_recv.at[seven], sq[0], sq[1], here).wait()
        inverse = lax.rsqrt(jnp.sum(sq_recv[...], axis=0) / D + EPS)
        inverse = jnp.broadcast_to(inverse[:1], (rows, NODES * rows))
        lane = n * rows + iota((rows, NODES * rows), 0)
        inverse = jnp.where(iota((rows, NODES * rows), 1) == lane, inverse, 0.0)
        inverse = jnp.sum(inverse, axis=1, keepdims=True)
        rd, re = gu_bufs[3], gu_bufs[4]
        total = gu[n].astype(F32) + rd[...].astype(F32) + re[0].astype(F32) + re[1].astype(F32)
        total *= inverse
        gate, up = total[:, :HID], total[:, HID:]
        hidden[n] = (gate / (1.0 + jnp.exp(-gate)) * up).astype(BF16)
        yield from gather8(hidden, node, sems, here)
        if only:
            loads[7].wait()
        product = dot(hidden[...].reshape(NODES * rows, HID), wd[...]).astype(BF16)
        yield from halves(product, part2, pair2, summed2)
        yield from scatter1(summed2, got2, chip, lambda to: (n, to * 2 + core), sems, here)
        total = jnp.sum(got2[...].astype(F32), axis=0)
        last[core] = (mixed[core, chip].astype(F32) + total).astype(BF16)
        recv = sems.take(1)[0]
        sems.start(last.at[core], last.at[core], recv, sibling)
        yield
        arrived(last.at[1 - core], recv, here)
        done[:, :HALF] = last[0].astype(F32)
        done[:, HALF:] = last[1, :, HALF - OFFSET :].astype(F32)

    both = pl.ds(0, DEVS - 1)
    running = {}

    def begin(j):
        for k, (which, steps) in enumerate(CHAINS):
            if which == j:
                context = send_context(j, steps, bufs[k], sems[k])
                running["abcdef"[k]] = (chain(j, steps, bufs[k], sems[k], context, k == 0), sems[k])

    def sort_tiles():
        rcopy(tiles.at[both], r1.at[both], far.at[0], far.at[1], here).wait()

        def sort(o, c):
            s2[o] = r1[dest_s[o]]
            return c

        lax.fori_loop(0, DEVS, sort, 0)

        def deliver(i, c):
            p = lax.rem(me + i, DEVS)
            rcopy(s2.at[p], r2.at[me], far.at[2], far.at[3], (p // LOCALS, lax.rem(p, LOCALS))).start()
            return c

        lax.fori_loop(1, DEVS, deliver, 0)
        r2[me] = s2[me]

    def attend_moved():
        rcopy(s2.at[both], r2.at[both], far.at[2], far.at[3], here).wait()
        for s in range(STEPS):
            for hb in range(blocks):
                for cb in range(5):
                    at = s * HEADS + hb * 16
                    query_arr[at : at + 16, cb * 128 : cb * 128 + 128] = r2[(s * blocks + hb) * 5 + cb]
        for cb in range(5):
            fresh[1, :, cb * 128 : cb * 128 + 128] = r2[STEPS * blocks * 5 + cb]
        attention(1)
        begin(1)

    loads[1].wait()
    attention(0)
    pl.semaphore_wait(barrier, NODES - 1 + LOCALS - 1)
    lax.fori_loop(1, LOCALS, greet_all, 0)
    begin(0)
    pl.semaphore_wait(ready, LOCALS - 1)
    lax.fori_loop(1, DEVS, spread, 0)

    def advance(name):
        steps, held = running[name]
        held.settle()
        try:
            next(steps)
        except StopIteration:
            del running[name]

    for name in ORDER:
        if name == "1":
            sort_tiles()
        elif name == "2":
            attend_moved()
        elif name in running:
            advance(name)
    while running:
        for name in list(running):
            advance(name)

    slot = slots(LOCALS, lambda row: chip * LOCALS + core * 8 + row // 2)
    pick = select(
        LOCALS, LOCALS,
        lambda row, column: (lax.rem(column, 8) == row // 2) & ((lax.rem(row, 2) == slot) == (column >= 8)),
    )
    at = pl.multiple_of(core * 8, 8)
    for s in range(STEPS):
        rows = [
            bufs[k][-1][pl.ds(steps.index(s) * LOCALS + at, 8), :]
            for j in range(2)
            for k, (which, steps) in enumerate(CHAINS)
            if which == j and s in steps
        ]
        out[s] = dot(pick, jnp.concatenate(rows, axis=0).astype(BF16)).astype(BF16)
    for held in sems:
        held.settle()
        held.settle()
        assert held.used <= RECEIVERS and senders.used <= SENDERS


CHAINS = ((0, (0,)), (0, (1, 2)), (1, (0,)), (1, (1, 2)))
SENDERS, RECEIVERS = 36, 29
ORDER = "ab1abab2ababcd"


def local(
    cache_pool, block_table, lengths, mig_slot, mig_dest, queries, new_entries, residual,
    w_uv, w_out, norm_gain, w_gate, w_up, w_down,
):
    by_slot = queries.reshape(STEPS * 2, HEADS, WIDTH)
    vm = pl.BlockSpec(memory_space=pltpu.VMEM)
    hbm = pl.BlockSpec(memory_space=pl.ANY)
    smem = pl.BlockSpec(memory_space=pltpu.SMEM)
    dma = pltpu.SemaphoreType.DMA
    V = pltpu.VMEM
    tile = (DEVS, 16, 128)
    return pl.pallas_call(
        kernel,
        out_shape=jax.ShapeDtypeStruct((STEPS, LOCALS, COLS), BF16),
        in_specs=[smem] * 4 + [vm] * 4 + [hbm] * 8,
        out_specs=vm,
        scratch_shapes=[
            V((STEPS * 2, HEADS, WIDTH), BF16), V((4, WIDTH, 256), BF16), V((STEPS, 64, COLS), BF16),
            V((8, LATENT, 128), BF16), V((1024, COLS), BF16), V((COLS, HID), BF16), V((COLS, HID), BF16),
            V((HID, COLS), BF16),
            V(tile, BF16), V(tile, BF16), V(tile, BF16), V(tile, BF16),
            V((STEPS * HEADS, KEYS), BF16), V((2, 16, KEYS), BF16), V((2, STEPS * HEADS, LATENT), F32),
            *[shape for _, steps in CHAINS for shape in chain_shapes(len(steps))],
            dma((8,)), pltpu.SemaphoreType.REGULAR, dma((4,)), dma((SENDERS,)), *[dma((RECEIVERS,)) for _ in CHAINS],
        ],
        compiler_params=pltpu.CompilerParams(
            collective_id=0, has_side_effects=True, vmem_limit_bytes=60 * 2**20
        ),
        name="layer",
    )(
        block_table, lengths, mig_slot, mig_dest, mig_slot.reshape(1, DEVS), mig_dest.reshape(1, DEVS),
        norm_gain, new_entries,
        by_slot, cache_pool, residual, w_uv, w_out, w_gate, w_up, w_down,
    )


def solution(mesh):
    in_specs = (
        P(("node", "local"), None, None),
        P(("node", "local"), None),
        P(),
        P(),
        P(),
        P(None, ("node", "local"), None),
        P(None, ("node", "local"), None),
        P(None, None, "node"),
        P("local", None, None),
        P("local", "node"),
        P("node"),
        P("node", "local"),
        P("node", "local"),
        P("local", "node"),
    )
    out_specs = P(None, "local", "node")
    return jax.shard_map(local, mesh=mesh, in_specs=in_specs, out_specs=out_specs, check_vma=False)
```

```python
import jax
import jax.numpy as jnp
from jax import lax
from jax.experimental import pallas as pl
from jax.experimental.pallas import tpu as pltpu
from jax.sharding import PartitionSpec as P

MESH = pl.DeviceIdType.MESH
BF16, F32 = jnp.bfloat16, jnp.float32
D = 7168
QK_NOPE = 128
LATENT = 512
ROPE = 64
WIDTH = LATENT + ROPE
STEPS = 3
HEADS = 128
NODES, LOCALS = 8, 16
DEVS = NODES * LOCALS
EPS = 1e-06
SCALE = (QK_NOPE + ROPE) ** (-0.5)
COLS = 896
HALF = 512
OFFSET = COLS - HALF
HID = 1152
KEYS = 640
NT = (((1,), (1,)), ((), ()))


def dot(a, b):
    return jnp.dot(a, b, preferred_element_type=F32)


def dot_nt(a, b):
    return lax.dot_general(a, b, NT, preferred_element_type=F32)


def iota(shape, dim):
    return lax.broadcasted_iota(jnp.int32, shape, dim)


def rcopy(src, dst, send, recv, device):
    return pltpu.make_async_remote_copy(
        src_ref=src, dst_ref=dst, send_sem=send, recv_sem=recv, device_id=device, device_id_type=MESH
    )


def attend(query, fresh, key0, key1, length):
    s0 = dot(query, key0) * SCALE
    s1 = dot(query, key1) * SCALE
    sf = dot_nt(query, fresh) * SCALE
    rows, block = s0.shape
    column = iota((rows, block), 1)
    s0 = jnp.where(column < length, s0, -jnp.inf)
    s1 = jnp.where(column + block < length, s1, -jnp.inf)
    step = iota(sf.shape, 0) // HEADS
    sf = jnp.where(iota(sf.shape, 1) <= step, sf, -jnp.inf)
    top = jnp.maximum(
        jnp.max(jnp.maximum(s0, s1), axis=1, keepdims=True), jnp.max(sf, axis=1, keepdims=True)
    )
    w0 = jnp.exp(s0 - top)
    w1 = jnp.exp(s1 - top)
    wf = jnp.exp(sf - top)
    total = jnp.sum(w0 + w1, axis=1, keepdims=True) + jnp.sum(wf, axis=1, keepdims=True)
    context = dot_nt(w0.astype(BF16), key0[:LATENT])
    context += dot_nt(w1.astype(BF16), key1[:LATENT])
    context += dot(wf.astype(BF16), fresh[:, :LATENT])
    return context / total


class Group:
    def __init__(self, pair, ring, block, device):
        self.p, self.r = pair, ring
        self.q = 1 - pair
        self.up, self.dn, self.op = lax.rem(ring + 1, 4), lax.rem(ring + 3, 4), lax.rem(ring + 2, 4)
        self.block, self.device = block, device


class Pool:
    def __init__(self, ref):
        self.ref, self.free, self.used = ref, [], 0

    def take(self):
        if self.free:
            return self.free.pop()
        self.used += 1
        return self.used - 1


class Sems:
    def __init__(self, ref, pool):
        self.ref, self.pool, self.used, self.sent, self.older = ref, pool, 0, [], []

    def take(self, count):
        first = self.used
        self.used += count
        return [self.ref.at[first + i] for i in range(count)]

    def sender(self):
        index = self.pool.take()
        return index, self.pool.ref.at[index]

    def keep(self, index, copy):
        self.sent.append((index, copy))

    def start(self, src, dst, recv, device):
        index, send = self.sender()
        copy = rcopy(src, dst, send, recv, device)
        copy.start()
        self.keep(index, copy)

    def settle(self):
        for index, copy in self.older:
            copy.wait_send()
            self.pool.free.append(index)
        self.older, self.sent = self.sent, []


def arrived(ref, recv, here):
    rcopy(ref, ref, recv, recv, here).wait_recv()


def gather8(buf, g, sems, here):
    width = buf.shape[-1] // 256 * 128
    lo, hi = pl.ds(0, width), pl.ds(width, buf.shape[-1] - width)
    recv = sems.take(5)
    b = g.block

    def send(block, to, index, cols=None):
        ref = buf.at[block] if cols is None else buf.at[block, :, cols]
        sems.start(ref, ref, recv[index], g.device(*to))

    own = b(g.p, g.r)
    send(own, (g.p, g.up), 1)
    send(own, (g.p, g.dn), 0)
    send(own, (g.q, g.r), 2)
    yield
    arrived(buf.at[b(g.p, g.up)], recv[0], here)
    send(b(g.p, g.up), (g.p, g.dn), 3, lo)
    arrived(buf.at[b(g.p, g.dn)], recv[1], here)
    send(b(g.p, g.dn), (g.p, g.up), 3, hi)
    arrived(buf.at[b(g.q, g.r)], recv[2], here)
    send(b(g.q, g.r), (g.p, g.up), 4)
    send(b(g.q, g.r), (g.p, g.dn), 4)
    yield
    arrived(buf.at[b(g.p, g.op)], recv[3], here)
    send(b(g.p, g.op), (g.q, g.r), 4)
    yield
    arrived(buf.at[pl.ds(0, 3)], recv[4], here)


def gather2(buf, g, sems, here):
    recv = sems.take(3)
    rings = (g.up, g.dn, g.op)

    def send(block, index, *to):
        sems.start(buf.at[block], buf.at[block], recv[index], g.device(*to))

    own, other = g.block(g.p, g.r), g.block(g.q, g.r)
    send(own, 0, g.q, g.r)
    for ring in rings:
        send(own, 1, g.p, ring)
    yield
    arrived(buf.at[other], recv[0], here)
    for ring in rings:
        send(other, 2, g.p, ring)
    yield
    arrived(buf.at[pl.ds(0, 3)], recv[1], here)
    arrived(buf.at[pl.ds(0, 3)], recv[2], here)


def scatter8(part, g, sems, here, meanwhile, ra, rb, rc, rd, re, sc, sd, se):
    width = part.shape[-1] // 2
    halves = (pl.ds(0, width), pl.ds(width, width))
    recv = sems.take(5)
    b = g.block

    def wide(ref, *at):
        return ref[at].astype(F32)

    sems.start(part.at[b(g.q, g.op)], ra, recv[0], g.device(g.q, g.r))
    sems.start(part.at[b(g.q, g.up)], rb.at[0], recv[1], g.device(g.p, g.up))
    sems.start(part.at[b(g.q, g.dn)], rb.at[1], recv[1], g.device(g.p, g.dn))
    meanwhile()
    up, dn = b(g.p, g.up), b(g.p, g.dn)
    yield
    arrived(ra, recv[0], here)
    sc[...] = (wide(part, b(g.p, g.op)) + wide(ra, ...)).astype(BF16)
    sems.start(sc.at[:, halves[0]], rc.at[0], recv[2], g.device(g.p, g.up))
    sems.start(sc.at[:, halves[1]], rc.at[1], recv[2], g.device(g.p, g.dn))
    sems.start(part.at[up, :, halves[1]], re.at[0, :, halves[1]], recv[4], g.device(g.p, g.up))
    sems.start(part.at[dn, :, halves[0]], re.at[1, :, halves[0]], recv[4], g.device(g.p, g.dn))
    arrived(rb, recv[1], here)
    sd[...] = (wide(part, b(g.q, g.r)) + wide(rb, 0) + wide(rb, 1)).astype(BF16)
    sems.start(sd, rd, recv[3], g.device(g.q, g.r))
    yield
    arrived(rc, recv[2], here)
    se[0] = (wide(part, up, slice(None), halves[0]) + wide(rc, 0)).astype(BF16)
    sems.start(se.at[0], re.at[0, :, halves[0]], recv[4], g.device(g.p, g.up))
    se[1] = (wide(part, dn, slice(None), halves[1]) + wide(rc, 1)).astype(BF16)
    sems.start(se.at[1], re.at[1, :, halves[1]], recv[4], g.device(g.p, g.dn))
    yield
    arrived(rd, recv[3], here)
    arrived(re, recv[4], here)


def ring_scatter(part, got, away, g, sems, here):
    recv = sems.take(1)[0]
    for i, ring in enumerate((g.up, g.dn, g.op)):
        sems.start(part.at[pl.ds(ring * 2, 2)], got.at[i], recv, g.device(g.p, ring))
    yield
    arrived(got, recv, here)
    terms = [part[pl.ds(g.r * 2, 2)]] + [got[i] for i in range(3)]
    away[...] = sum(t.astype(F32) for t in terms).astype(BF16)


def scatter1(part, got, own, device, sems, here):
    recv = sems.take(1)[0]
    index, send = sems.sender()

    def spread(i, c):
        to = lax.rem(own + i, 8)
        rcopy(part.at[to], got.at[own], send, recv, device(to)).start()
        return c

    lax.fori_loop(1, 8, spread, 0)
    got[own] = part[own]
    seven = pl.ds(0, 7)
    sems.keep(index, rcopy(part.at[seven], got.at[seven], send, recv, here))
    yield
    rcopy(part.at[seven], got.at[seven], send, recv, here).wait_recv()


def ring_shapes(rows, cols):
    V = pltpu.VMEM
    return [V((3, 2, rows, cols), BF16), V((2, rows, cols), BF16), V((2, rows, cols), BF16)]


def scatter8_shapes(rows, cols):
    V = pltpu.VMEM
    return [
        V((rows, cols), BF16), V((2, rows, cols), BF16), V((2, rows, cols // 2), BF16),
        V((rows, cols), BF16), V((2, rows, cols), BF16), V((rows, cols), BF16),
        V((rows, cols), BF16), V((2, rows, cols // 2), BF16),
    ]


def chain_shapes(steps):
    V = pltpu.VMEM
    rows = LOCALS * steps
    return [
        V((LOCALS, rows, 256), BF16), V((LOCALS, rows, 256), BF16), V((LATENT // 128, 8 * rows, 128), F32),
        V((NODES, rows, 1024), BF16), V((NODES, rows, COLS), BF16),
        V((NODES, rows, HALF), BF16), V((NODES, rows, HALF), BF16), V((2, NODES, rows, HALF), BF16),
        *ring_shapes(rows, HALF),
        V((NODES, rows, 2 * HID), BF16), V((8, NODES * rows), F32), V((NODES, 8, NODES * rows), F32),
        V((NODES, rows, HID), BF16),
        *scatter8_shapes(rows, 2 * HID),
        V((NODES, rows, COLS), BF16), V((NODES, rows, HALF), BF16), V((NODES, rows, HALF), BF16),
        V((NODES, rows, HALF), BF16), V((2, rows, HALF), BF16), V((rows, COLS), F32),
    ]


def kernel(
    table, lengths, slot_s, dest_s, slot_v, dest_v, gain, fresh_all,
    query_hbm, pool_hbm, resid_hbm, wuv_hbm, wout_hbm, wg_hbm, wu_hbm, wd_hbm,
    out, *scratch,
):
    refs = list(scratch)
    take = lambda count=1: [refs.pop(0) for _ in range(count)]
    query, pool, resid, wuv, wout, wg, wu, wd = take(8)
    tiles, r1, s2, r2, query_arr, fresh, ctx = take(7)
    bufs = [take(len(chain_shapes(1))) for _ in CHAINS]
    wsem, ready, far, senders = take(4)
    senders = Pool(senders)
    sems = [Sems(ref, senders) for ref in take(len(CHAINS))]

    n, l = lax.axis_index("node"), lax.axis_index("local")
    me = n * LOCALS + l
    here = (n, l)
    core, chip = lax.rem(l, 2), l // 2
    sibling = (n, l + 1 - 2 * core)
    mine = pl.multiple_of(core * OFFSET, 128)
    theirs = pl.multiple_of((1 - core) * OFFSET, 128)
    node = Group(n // 4, lax.rem(n, 4), lambda p, r: p * 4 + r, lambda p, r: (p * 4 + r, l))
    chips = Group(
        lax.rem(chip, 2), chip // 2, lambda p, r: r * 2 + p, lambda p, r: (n, (r * 2 + p) * 2 + core)
    )

    barrier = pltpu.get_barrier_semaphore()

    def greet_node(i, c):
        pl.semaphore_signal(barrier, inc=1, device_id=(lax.rem(n + i, NODES), l), device_id_type=MESH)
        return c

    def greet_local(i, c):
        pl.semaphore_signal(barrier, inc=1, device_id=(n, lax.rem(l + i, LOCALS)), device_id_type=MESH)
        return c

    def greet_all(i, c):
        pl.semaphore_signal(ready, inc=1, device_id=(n, lax.rem(l + i, LOCALS)), device_id_type=MESH)
        return c

    lax.fori_loop(1, NODES, greet_node, 0)
    lax.fori_loop(1, LOCALS, greet_local, 0)

    loads = [
        pltpu.make_async_copy(a, b, wsem.at[i])
        for i, (a, b) in enumerate(
            (
                (query_hbm, query), (pool_hbm, pool), (wuv_hbm, wuv), (wout_hbm, wout),
                (resid_hbm.at[:, pl.ds(chip // 2 * 64, 64), :], resid),
                (wg_hbm, wg), (wu_hbm, wu), (wd_hbm, wd),
            )
        )
    ]
    for copy in loads:
        copy.start()

    gain_row = gain[...].reshape(1, COLS)
    leave = slot_s[me]
    stay = 1 - leave

    fresh[...] = jnp.zeros(fresh.shape, BF16)
    both_fresh = fresh_all[...].astype(F32)
    fresh[0, :STEPS, :WIDTH] = jnp.where(stay == 0, both_fresh[:, 0], both_fresh[:, 1]).astype(BF16)
    fresh[1, :STEPS, :WIDTH] = jnp.where(stay == 1, both_fresh[:, 0], both_fresh[:, 1]).astype(BF16)
    loads[0].wait()
    blocks = HEADS // 16
    for s in range(STEPS):
        for hb in range(blocks):
            for cb in range(5):
                width = min(128, WIDTH - cb * 128)
                tiles[(s * blocks + hb) * 5 + cb, :, :width] = query[
                    s * 2 + leave, hb * 16 : hb * 16 + 16, cb * 128 : cb * 128 + width
                ]
    for cb in range(5):
        tiles[STEPS * blocks * 5 + cb] = fresh[1, :, cb * 128 : cb * 128 + 128]

    def spread(i, c):
        p = lax.rem(me + i, DEVS)
        rcopy(tiles.at[p], r1.at[me], far.at[0], far.at[1], (p // LOCALS, lax.rem(p, LOCALS))).start()
        return c

    r1[me] = tiles[me]

    def attention(j):
        if j == 0:
            request, new = stay, fresh[0, :, :WIDTH]
            rows = jnp.concatenate([query[s * 2 + stay] for s in range(STEPS)], axis=0)
        else:
            request, new = leave, fresh[1, :, :WIDTH]
            rows = query_arr[:, :WIDTH]
        key0, key1 = pool[table[request, 0]], pool[table[request, 1]]
        ctx[j] = attend(rows, new, key0, key1, lengths[me * 2 + request])

    others = pl.ds(0, LOCALS - 1)

    def send_context(j, steps, bufs, sems):
        ctx_send, ctx_recv = bufs[:2]

        def group(g):
            at = pl.multiple_of(g * 8, 8)
            rows = jnp.concatenate([ctx[j, pl.ds(s * HEADS + at, 8), :] for s in steps], axis=0)
            return jnp.concatenate([rows[:, :256], rows[:, 256:]], axis=0).astype(BF16)

        send, recv = sems.take(2)

        def send_group(i, c):
            g = lax.rem(l + i, LOCALS)
            ctx_send[g] = group(g)
            rcopy(ctx_send.at[g], ctx_recv.at[l], send, recv, (n, g)).start()
            return c

        lax.fori_loop(1, LOCALS, send_group, 0)
        ctx_recv[l] = group(l)
        return rcopy(ctx_send.at[others], ctx_recv.at[others], send, recv, here)

    def select(rows, columns, test):
        return jnp.where(test(iota((rows, columns), 0), iota((rows, columns), 1)), 1.0, 0.0).astype(BF16)

    def slots(rows, device):
        lanes = jnp.broadcast_to(slot_v[...], (rows, DEVS)).astype(F32)
        at = device(iota((rows, DEVS), 0)) == iota((rows, DEVS), 1)
        return jnp.sum(jnp.where(at, lanes, 0.0), axis=1, keepdims=True).astype(jnp.int32)

    def chain(j, steps, bufs, sems, context, only):
        count = len(steps)
        rows = LOCALS * count
        bufs = list(bufs)
        take = lambda count=1: [bufs.pop(0) for _ in range(count)]
        ctx_send, ctx_recv, wide, values, part, pair, summed, mixed = take(8)
        got, away, back = take(3)
        gu, sq_send, sq_recv, hidden = take(4)
        gu_bufs = take(8)
        part2, pair2, summed2 = take(3)
        got2 = take()[0]
        last, done = take(2)

        def halves(product, part, pair, summed):
            part[...] = product.reshape(NODES, rows, COLS)
            recv = sems.take(1)[0]
            sems.start(part.at[:, :, pl.ds(theirs, HALF)], pair, recv, sibling)
            yield
            arrived(pair, recv, here)
            summed[...] = (part[:, :, pl.ds(mine, HALF)].astype(F32) + pair[...].astype(F32)).astype(BF16)

        if only:
            loads[2].wait()
        context.wait()
        for t in range(2):
            recv = ctx_recv[:, :, t * 128 : t * 128 + 128].astype(F32)
            for half in range(2):
                for s in range(count):
                    at = (half * count + s) * 8
                    wide[half * 2 + t, s * 128 : s * 128 + 128] = recv[:, at : at + 8].reshape(128, 128)
        for h in range(8):
            head = [wide[t, pl.ds(h, rows, stride=8), :] for t in range(LATENT // 128)]
            head = jnp.concatenate(head, axis=1).astype(BF16)
            values[n, :, h * 128 : h * 128 + 128] = dot(head, wuv[h]).astype(BF16)
        yield from GATHER[VALUES[j]](values, node, sems, here)
        if only:
            loads[3].wait()
        product = dot(values[...].reshape(NODES * rows, 1024), wout[...]).astype(BF16)
        if j == 1:
            pick = select(DEVS, DEVS, lambda row, column: dest_v[...] == row)
            by_step = product.reshape(NODES, count, LOCALS, COLS)
            moved = [dot(pick, by_step[:, s].reshape(DEVS, COLS)).astype(BF16) for s in range(count)]
            product = jnp.concatenate([m.reshape(NODES, LOCALS, COLS) for m in moved], axis=1)
        yield from halves(product, part, pair, summed)

        yield from ring_scatter(summed, got, away, chips, sems, here)
        recv = sems.take(1)[0]
        sems.start(away, back, recv, chips.device(chips.q, chips.r))
        if only:
            loads[4].wait()
        slot = slots(2 * LOCALS, lambda row: chips.r * 2 * LOCALS + row)
        pick = select(
            2 * LOCALS, 4 * LOCALS,
            lambda row, column: (column // 2 == row) & ((lax.rem(column, 2) == slot) == (j == 1)),
        )
        skip = [dot(pick, resid[s, :, pl.ds(mine, HALF)]) for s in steps]
        skip = jnp.concatenate([k.reshape(2, LOCALS, HALF) for k in skip], axis=1)
        yield
        arrived(back, recv, here)
        two = pl.ds(chips.r * 2, 2)
        mixed[core, two] = (skip + (away[...].astype(F32) + back[...].astype(F32))).astype(BF16)

        side = sems.take(1)[0]
        recv = sems.take(3)

        def pass_on(ring):
            ref = mixed.at[core, pl.ds(ring * 2, 2)]
            sems.start(ref, ref, side, sibling)

        for i, ring in enumerate((chips.up, chips.dn, chips.op)):
            ref = mixed.at[core, two]
            sems.start(ref, ref, recv[i], chips.device(chips.p, ring))
        pass_on(chips.r)
        yield
        for i, ring in enumerate((chips.dn, chips.up, chips.op)):
            arrived(mixed.at[core, pl.ds(ring * 2, 2)], recv[i], here)
            pass_on(ring)
        arrived(mixed.at[1 - core], side, here)

        if only:
            loads[5].wait()
            loads[6].wait()
        sq = sems.take(2)

        left = mixed[0].reshape(NODES * rows, HALF).astype(F32)
        right = mixed[1, :, :, HALF - OFFSET :].reshape(NODES * rows, OFFSET).astype(F32)
        whole = jnp.concatenate([left, right], axis=1)
        scaled = (whole * gain_row).astype(BF16)
        gu[:, :, :HID] = dot(scaled, wg[...]).astype(BF16).reshape(NODES, rows, HID)
        gu[:, :, HID:] = dot(scaled, wu[...]).astype(BF16).reshape(NODES, rows, HID)

        def squares():
            square = whole * whole
            lanes = square[:, :128]
            for t in range(1, COLS // 128):
                lanes += square[:, t * 128 : t * 128 + 128]
            sq_send[...] = lax.dot_general(
                jnp.ones((8, 128), F32), lanes, NT, precision=lax.Precision.HIGHEST, preferred_element_type=F32
            )

            def send_sq(i, c):
                p = lax.rem(n + i, NODES)
                rcopy(sq_send, sq_recv.at[n], sq[0], sq[1], (p, l)).start()
                return c

            lax.fori_loop(1, NODES, send_sq, 0)
            sq_recv[n] = sq_send[...]

        yield from scatter8(gu, node, sems, here, squares, *gu_bufs)
        seven = pl.ds(0, NODES - 1)
        rcopy(sq_recv.at[seven], sq_recv.at[seven], sq[0], sq[1], here).wait()
        inverse = lax.rsqrt(jnp.sum(sq_recv[...], axis=0) / D + EPS)
        inverse = jnp.broadcast_to(inverse[:1], (rows, NODES * rows))
        lane = n * rows + iota((rows, NODES * rows), 0)
        inverse = jnp.where(iota((rows, NODES * rows), 1) == lane, inverse, 0.0)
        inverse = jnp.sum(inverse, axis=1, keepdims=True)
        rd, re = gu_bufs[3], gu_bufs[4]
        total = gu[n].astype(F32) + rd[...].astype(F32) + re[0].astype(F32) + re[1].astype(F32)
        total *= inverse
        gate, up = total[:, :HID], total[:, HID:]
        hidden[n] = (gate / (1.0 + jnp.exp(-gate)) * up).astype(BF16)
        yield from GATHER[HIDDEN[j]](hidden, node, sems, here)
        if only:
            loads[7].wait()
        product = dot(hidden[...].reshape(NODES * rows, HID), wd[...]).astype(BF16)
        yield from halves(product, part2, pair2, summed2)
        yield from scatter1(summed2, got2, chip, lambda to: (n, to * 2 + core), sems, here)
        total = jnp.sum(got2[...].astype(F32), axis=0)
        last[core] = (mixed[core, chip].astype(F32) + total).astype(BF16)
        recv = sems.take(1)[0]
        sems.start(last.at[core], last.at[core], recv, sibling)
        yield
        arrived(last.at[1 - core], recv, here)
        done[:, :HALF] = last[0].astype(F32)
        done[:, HALF:] = last[1, :, HALF - OFFSET :].astype(F32)

    both = pl.ds(0, DEVS - 1)
    running = {}

    def begin(j):
        for k, (which, steps) in enumerate(CHAINS):
            if which == j:
                context = send_context(j, steps, bufs[k], sems[k])
                running["abcdef"[k]] = (chain(j, steps, bufs[k], sems[k], context, k == 0), sems[k])

    def advance(name):
        steps, held = running[name]
        held.settle()
        try:
            next(steps)
        except StopIteration:
            del running[name]

    def sort_tiles():
        rcopy(tiles.at[both], r1.at[both], far.at[0], far.at[1], here).wait()

        def sort(o, c):
            s2[o] = r1[dest_s[o]]
            return c

        lax.fori_loop(0, DEVS, sort, 0)

        def deliver(i, c):
            p = lax.rem(me + i, DEVS)
            rcopy(s2.at[p], r2.at[me], far.at[2], far.at[3], (p // LOCALS, lax.rem(p, LOCALS))).start()
            return c

        lax.fori_loop(1, DEVS, deliver, 0)
        r2[me] = s2[me]

    def attend_moved():
        rcopy(s2.at[both], r2.at[both], far.at[2], far.at[3], here).wait()
        for s in range(STEPS):
            for hb in range(blocks):
                for cb in range(5):
                    at = s * HEADS + hb * 16
                    query_arr[at : at + 16, cb * 128 : cb * 128 + 128] = r2[(s * blocks + hb) * 5 + cb]
        for cb in range(5):
            fresh[1, :, cb * 128 : cb * 128 + 128] = r2[STEPS * blocks * 5 + cb]
        attention(1)
        begin(1)

    loads[1].wait()
    attention(0)
    pl.semaphore_wait(barrier, NODES - 1 + LOCALS - 1)
    lax.fori_loop(1, LOCALS, greet_all, 0)
    begin(0)
    pl.semaphore_wait(ready, LOCALS - 1)
    lax.fori_loop(1, DEVS, spread, 0)

    for name in ORDER:
        if name == "1":
            sort_tiles()
        elif name == "2":
            attend_moved()
        elif name in running:
            advance(name)
    while running:
        for name in list(running):
            advance(name)

    slot = slots(LOCALS, lambda row: chip * LOCALS + core * 8 + row // 2)
    pick = select(
        LOCALS, LOCALS,
        lambda row, column: (lax.rem(column, 8) == row // 2) & ((lax.rem(row, 2) == slot) == (column >= 8)),
    )
    at = pl.multiple_of(core * 8, 8)
    for s in range(STEPS):
        rows = [
            bufs[k][-1][pl.ds(steps.index(s) * LOCALS + at, 8), :]
            for j in range(2)
            for k, (which, steps) in enumerate(CHAINS)
            if which == j and s in steps
        ]
        out[s] = dot(pick, jnp.concatenate(rows, axis=0).astype(BF16)).astype(BF16)
    for held in sems:
        held.settle()
        held.settle()
        assert held.used <= RECEIVERS and senders.used <= SENDERS


CHAINS = ((0, (0,)), (0, (1,)), (0, (2,)), (1, (0,)), (1, (1,)), (1, (2,)))
SENDERS, RECEIVERS = 51, 29
GATHER = {"three": gather8, "two": gather2}
VALUES = ("three", "three")
HIDDEN = ("three", "two")
ORDER = "abcabc1abc2abcabcdef"


def local(
    cache_pool, block_table, lengths, mig_slot, mig_dest, queries, new_entries, residual,
    w_uv, w_out, norm_gain, w_gate, w_up, w_down,
):
    by_slot = queries.reshape(STEPS * 2, HEADS, WIDTH)
    vm = pl.BlockSpec(memory_space=pltpu.VMEM)
    hbm = pl.BlockSpec(memory_space=pl.ANY)
    smem = pl.BlockSpec(memory_space=pltpu.SMEM)
    dma = pltpu.SemaphoreType.DMA
    V = pltpu.VMEM
    tile = (DEVS, 16, 128)
    return pl.pallas_call(
        kernel,
        out_shape=jax.ShapeDtypeStruct((STEPS, LOCALS, COLS), BF16),
        in_specs=[smem] * 4 + [vm] * 4 + [hbm] * 8,
        out_specs=vm,
        scratch_shapes=[
            V((STEPS * 2, HEADS, WIDTH), BF16), V((4, WIDTH, 256), BF16), V((STEPS, 64, COLS), BF16),
            V((8, LATENT, 128), BF16), V((1024, COLS), BF16), V((COLS, HID), BF16), V((COLS, HID), BF16),
            V((HID, COLS), BF16),
            V(tile, BF16), V(tile, BF16), V(tile, BF16), V(tile, BF16),
            V((STEPS * HEADS, KEYS), BF16), V((2, 16, KEYS), BF16), V((2, STEPS * HEADS, LATENT), F32),
            *[shape for _, steps in CHAINS for shape in chain_shapes(len(steps))],
            dma((8,)), pltpu.SemaphoreType.REGULAR, dma((4,)), dma((SENDERS,)), *[dma((RECEIVERS,)) for _ in CHAINS],
        ],
        compiler_params=pltpu.CompilerParams(
            collective_id=0, has_side_effects=True, vmem_limit_bytes=60 * 2**20
        ),
        name="layer",
    )(
        block_table, lengths, mig_slot, mig_dest, mig_slot.reshape(1, DEVS), mig_dest.reshape(1, DEVS),
        norm_gain, new_entries,
        by_slot, cache_pool, residual, w_uv, w_out, w_gate, w_up, w_down,
    )


def solution(mesh):
    in_specs = (
        P(("node", "local"), None, None),
        P(("node", "local"), None),
        P(),
        P(),
        P(),
        P(None, ("node", "local"), None),
        P(None, ("node", "local"), None),
        P(None, None, "node"),
        P("local", None, None),
        P("local", "node"),
        P("node"),
        P("node", "local"),
        P("node", "local"),
        P("local", "node"),
    )
    out_specs = P(None, "local", "node")
    return jax.shard_map(local, mesh=mesh, in_specs=in_specs, out_specs=out_specs, check_vma=False)
```

```python
import jax
import jax.numpy as jnp
from jax import lax
from jax.experimental import pallas as pl
from jax.experimental.pallas import tpu as pltpu
from jax.sharding import PartitionSpec as P

MESH = pl.DeviceIdType.MESH
BF16, F32 = jnp.bfloat16, jnp.float32
D = 7168
QK_NOPE = 128
LATENT = 512
ROPE = 64
WIDTH = LATENT + ROPE
STEPS = 3
HEADS = 128
NODES, LOCALS = 8, 16
DEVS = NODES * LOCALS
EPS = 1e-06
SCALE = (QK_NOPE + ROPE) ** (-0.5)
COLS = 896
HALF = 512
OFFSET = COLS - HALF
HID = 1152
KEYS = 640
NT = (((1,), (1,)), ((), ()))


def dot(a, b):
    return jnp.dot(a, b, preferred_element_type=F32)


def dot_nt(a, b):
    return lax.dot_general(a, b, NT, preferred_element_type=F32)


def iota(shape, dim):
    return lax.broadcasted_iota(jnp.int32, shape, dim)


def rcopy(src, dst, send, recv, device):
    return pltpu.make_async_remote_copy(
        src_ref=src, dst_ref=dst, send_sem=send, recv_sem=recv, device_id=device, device_id_type=MESH
    )


def attend(query, fresh, key0, key1, length):
    s0 = dot(query, key0) * SCALE
    s1 = dot(query, key1) * SCALE
    sf = dot_nt(query, fresh) * SCALE
    rows, block = s0.shape
    column = iota((rows, block), 1)
    s0 = jnp.where(column < length, s0, -jnp.inf)
    s1 = jnp.where(column + block < length, s1, -jnp.inf)
    step = iota(sf.shape, 0) // HEADS
    sf = jnp.where(iota(sf.shape, 1) <= step, sf, -jnp.inf)
    top = jnp.maximum(
        jnp.max(jnp.maximum(s0, s1), axis=1, keepdims=True), jnp.max(sf, axis=1, keepdims=True)
    )
    w0 = jnp.exp(s0 - top)
    w1 = jnp.exp(s1 - top)
    wf = jnp.exp(sf - top)
    total = jnp.sum(w0 + w1, axis=1, keepdims=True) + jnp.sum(wf, axis=1, keepdims=True)
    context = dot_nt(w0.astype(BF16), key0[:LATENT])
    context += dot_nt(w1.astype(BF16), key1[:LATENT])
    context += dot(wf.astype(BF16), fresh[:, :LATENT])
    return context / total


class Group:
    def __init__(self, pair, ring, block, device):
        self.p, self.r = pair, ring
        self.q = 1 - pair
        self.up, self.dn, self.op = lax.rem(ring + 1, 4), lax.rem(ring + 3, 4), lax.rem(ring + 2, 4)
        self.block, self.device = block, device


class Pool:
    def __init__(self, ref):
        self.ref, self.free, self.used = ref, [], 0

    def take(self):
        if self.free:
            return self.free.pop()
        self.used += 1
        return self.used - 1


class Sems:
    def __init__(self, ref, pool):
        self.ref, self.pool, self.used, self.sent, self.older = ref, pool, 0, [], []

    def take(self, count):
        first = self.used
        self.used += count
        return [self.ref.at[first + i] for i in range(count)]

    def sender(self):
        index = self.pool.take()
        return index, self.pool.ref.at[index]

    def keep(self, index, copy):
        self.sent.append((index, copy))

    def start(self, src, dst, recv, device):
        index, send = self.sender()
        copy = rcopy(src, dst, send, recv, device)
        copy.start()
        self.keep(index, copy)

    def settle(self):
        for index, copy in self.older:
            copy.wait_send()
            self.pool.free.append(index)
        self.older, self.sent = self.sent, []


def arrived(ref, recv, here):
    rcopy(ref, ref, recv, recv, here).wait_recv()


def gather8(buf, g, sems, here):
    width = buf.shape[-1] // 256 * 128
    lo, hi = pl.ds(0, width), pl.ds(width, buf.shape[-1] - width)
    recv = sems.take(5)
    b = g.block

    def send(block, to, index, cols=None):
        ref = buf.at[block] if cols is None else buf.at[block, :, cols]
        sems.start(ref, ref, recv[index], g.device(*to))

    own = b(g.p, g.r)
    send(own, (g.p, g.up), 1)
    send(own, (g.p, g.dn), 0)
    send(own, (g.q, g.r), 2)
    yield
    arrived(buf.at[b(g.p, g.up)], recv[0], here)
    send(b(g.p, g.up), (g.p, g.dn), 3, lo)
    arrived(buf.at[b(g.p, g.dn)], recv[1], here)
    send(b(g.p, g.dn), (g.p, g.up), 3, hi)
    arrived(buf.at[b(g.q, g.r)], recv[2], here)
    send(b(g.q, g.r), (g.p, g.up), 4)
    send(b(g.q, g.r), (g.p, g.dn), 4)
    yield
    arrived(buf.at[b(g.p, g.op)], recv[3], here)
    send(b(g.p, g.op), (g.q, g.r), 4)
    yield
    arrived(buf.at[pl.ds(0, 3)], recv[4], here)


def gather2(buf, g, sems, here):
    recv = sems.take(3)
    rings = (g.up, g.dn, g.op)

    def send(block, index, *to):
        sems.start(buf.at[block], buf.at[block], recv[index], g.device(*to))

    own, other = g.block(g.p, g.r), g.block(g.q, g.r)
    send(own, 0, g.q, g.r)
    for ring in rings:
        send(own, 1, g.p, ring)
    yield
    arrived(buf.at[other], recv[0], here)
    for ring in rings:
        send(other, 2, g.p, ring)
    yield
    arrived(buf.at[pl.ds(0, 3)], recv[1], here)
    arrived(buf.at[pl.ds(0, 3)], recv[2], here)


def scatter8(part, g, sems, here, meanwhile, ra, rb, rc, rd, re, sc, sd, se):
    width = part.shape[-1] // 2
    halves = (pl.ds(0, width), pl.ds(width, width))
    recv = sems.take(5)
    b = g.block

    def wide(ref, *at):
        return ref[at].astype(F32)

    sems.start(part.at[b(g.q, g.op)], ra, recv[0], g.device(g.q, g.r))
    sems.start(part.at[b(g.q, g.up)], rb.at[0], recv[1], g.device(g.p, g.up))
    sems.start(part.at[b(g.q, g.dn)], rb.at[1], recv[1], g.device(g.p, g.dn))
    meanwhile()
    up, dn = b(g.p, g.up), b(g.p, g.dn)
    yield
    arrived(ra, recv[0], here)
    sc[...] = (wide(part, b(g.p, g.op)) + wide(ra, ...)).astype(BF16)
    sems.start(sc.at[:, halves[0]], rc.at[0], recv[2], g.device(g.p, g.up))
    sems.start(sc.at[:, halves[1]], rc.at[1], recv[2], g.device(g.p, g.dn))
    sems.start(part.at[up, :, halves[1]], re.at[0, :, halves[1]], recv[4], g.device(g.p, g.up))
    sems.start(part.at[dn, :, halves[0]], re.at[1, :, halves[0]], recv[4], g.device(g.p, g.dn))
    arrived(rb, recv[1], here)
    sd[...] = (wide(part, b(g.q, g.r)) + wide(rb, 0) + wide(rb, 1)).astype(BF16)
    sems.start(sd, rd, recv[3], g.device(g.q, g.r))
    yield
    arrived(rc, recv[2], here)
    se[0] = (wide(part, up, slice(None), halves[0]) + wide(rc, 0)).astype(BF16)
    sems.start(se.at[0], re.at[0, :, halves[0]], recv[4], g.device(g.p, g.up))
    se[1] = (wide(part, dn, slice(None), halves[1]) + wide(rc, 1)).astype(BF16)
    sems.start(se.at[1], re.at[1, :, halves[1]], recv[4], g.device(g.p, g.dn))
    yield
    arrived(rd, recv[3], here)
    arrived(re, recv[4], here)


def ring_scatter(part, got, away, g, sems, here):
    recv = sems.take(1)[0]
    for i, ring in enumerate((g.up, g.dn, g.op)):
        sems.start(part.at[pl.ds(ring * 2, 2)], got.at[i], recv, g.device(g.p, ring))
    yield
    arrived(got, recv, here)
    terms = [part[pl.ds(g.r * 2, 2)]] + [got[i] for i in range(3)]
    away[...] = sum(t.astype(F32) for t in terms).astype(BF16)


def scatter1(part, got, own, device, sems, here):
    recv = sems.take(1)[0]
    index, send = sems.sender()

    def spread(i, c):
        to = lax.rem(own + i, 8)
        rcopy(part.at[to], got.at[own], send, recv, device(to)).start()
        return c

    lax.fori_loop(1, 8, spread, 0)
    got[own] = part[own]
    seven = pl.ds(0, 7)
    sems.keep(index, rcopy(part.at[seven], got.at[seven], send, recv, here))
    yield
    rcopy(part.at[seven], got.at[seven], send, recv, here).wait_recv()


def ring_shapes(rows, cols):
    V = pltpu.VMEM
    return [V((3, 2, rows, cols), BF16), V((2, rows, cols), BF16), V((2, rows, cols), BF16)]


def scatter8_shapes(rows, cols):
    V = pltpu.VMEM
    return [
        V((rows, cols), BF16), V((2, rows, cols), BF16), V((2, rows, cols // 2), BF16),
        V((rows, cols), BF16), V((2, rows, cols), BF16), V((rows, cols), BF16),
        V((rows, cols), BF16), V((2, rows, cols // 2), BF16),
    ]


def chain_shapes(steps):
    V = pltpu.VMEM
    rows = LOCALS * steps
    return [
        V((LOCALS, rows, 256), BF16), V((LOCALS, rows, 256), BF16), V((LATENT // 128, 8 * rows, 128), F32),
        V((NODES, rows, 1024), BF16), V((NODES, rows, COLS), BF16),
        V((NODES, rows, HALF), BF16), V((NODES, rows, HALF), BF16), V((2, NODES, rows, HALF), BF16),
        *ring_shapes(rows, HALF),
        V((NODES, rows, 2 * HID), BF16), V((8, NODES * rows), F32), V((NODES, 8, NODES * rows), F32),
        V((NODES, rows, HID), BF16),
        *scatter8_shapes(rows, 2 * HID),
        V((NODES, rows, COLS), BF16), V((NODES, rows, HALF), BF16), V((NODES, rows, HALF), BF16),
        V((NODES, rows, HALF), BF16), V((2, rows, HALF), BF16), V((rows, COLS), F32),
    ]


def kernel(
    table, lengths, slot_s, dest_s, slot_v, dest_v, gain, fresh_all,
    query_hbm, pool_hbm, resid_hbm, wuv_hbm, wout_hbm, wg_hbm, wu_hbm, wd_hbm,
    out, *scratch,
):
    refs = list(scratch)
    take = lambda count=1: [refs.pop(0) for _ in range(count)]
    query, pool, resid, wuv, wout, wg, wu, wd = take(8)
    tiles, r1, s2, r2, query_arr, fresh, ctx = take(7)
    bufs = [take(len(chain_shapes(1))) for _ in CHAINS]
    wsem, ready, far, senders = take(4)
    senders = Pool(senders)
    sems = [Sems(ref, senders) for ref in take(len(CHAINS))]

    n, l = lax.axis_index("node"), lax.axis_index("local")
    me = n * LOCALS + l
    here = (n, l)
    core, chip = lax.rem(l, 2), l // 2
    sibling = (n, l + 1 - 2 * core)
    mine = pl.multiple_of(core * OFFSET, 128)
    theirs = pl.multiple_of((1 - core) * OFFSET, 128)
    node = Group(n // 4, lax.rem(n, 4), lambda p, r: p * 4 + r, lambda p, r: (p * 4 + r, l))
    chips = Group(
        lax.rem(chip, 2), chip // 2, lambda p, r: r * 2 + p, lambda p, r: (n, (r * 2 + p) * 2 + core)
    )

    barrier = pltpu.get_barrier_semaphore()

    def greet_node(i, c):
        pl.semaphore_signal(barrier, inc=1, device_id=(lax.rem(n + i, NODES), l), device_id_type=MESH)
        return c

    def greet_local(i, c):
        pl.semaphore_signal(barrier, inc=1, device_id=(n, lax.rem(l + i, LOCALS)), device_id_type=MESH)
        return c

    def greet_all(i, c):
        pl.semaphore_signal(ready, inc=1, device_id=(n, lax.rem(l + i, LOCALS)), device_id_type=MESH)
        return c

    lax.fori_loop(1, NODES, greet_node, 0)
    lax.fori_loop(1, LOCALS, greet_local, 0)

    loads = [
        pltpu.make_async_copy(a, b, wsem.at[i])
        for i, (a, b) in enumerate(
            (
                (query_hbm, query), (pool_hbm, pool), (wuv_hbm, wuv), (wout_hbm, wout),
                (resid_hbm.at[:, pl.ds(chip // 2 * 64, 64), :], resid),
                (wg_hbm, wg), (wu_hbm, wu), (wd_hbm, wd),
            )
        )
    ]
    for copy in loads[:2]:
        copy.start()

    gain_row = gain[...].reshape(1, COLS)
    leave = slot_s[me]
    stay = 1 - leave

    fresh[...] = jnp.zeros(fresh.shape, BF16)
    both_fresh = fresh_all[...].astype(F32)
    fresh[0, :STEPS, :WIDTH] = jnp.where(stay == 0, both_fresh[:, 0], both_fresh[:, 1]).astype(BF16)
    fresh[1, :STEPS, :WIDTH] = jnp.where(stay == 1, both_fresh[:, 0], both_fresh[:, 1]).astype(BF16)
    loads[0].wait()
    blocks = HEADS // 16
    for s in range(STEPS):
        for hb in range(blocks):
            for cb in range(5):
                width = min(128, WIDTH - cb * 128)
                tiles[(s * blocks + hb) * 5 + cb, :, :width] = query[
                    s * 2 + leave, hb * 16 : hb * 16 + 16, cb * 128 : cb * 128 + width
                ]
    for cb in range(5):
        tiles[STEPS * blocks * 5 + cb] = fresh[1, :, cb * 128 : cb * 128 + 128]

    def spread(i, c):
        p = lax.rem(me + i, DEVS)
        rcopy(tiles.at[p], r1.at[me], far.at[0], far.at[1], (p // LOCALS, lax.rem(p, LOCALS))).start()
        return c

    r1[me] = tiles[me]

    def attention(j):
        if j == 0:
            request, new = stay, fresh[0, :, :WIDTH]
            rows = jnp.concatenate([query[s * 2 + stay] for s in range(STEPS)], axis=0)
        else:
            request, new = leave, fresh[1, :, :WIDTH]
            rows = query_arr[:, :WIDTH]
        key0, key1 = pool[table[request, 0]], pool[table[request, 1]]
        ctx[j] = attend(rows, new, key0, key1, lengths[me * 2 + request])

    others = pl.ds(0, LOCALS - 1)

    def send_context(j, steps, bufs, sems):
        ctx_send, ctx_recv = bufs[:2]

        def group(g):
            at = pl.multiple_of(g * 8, 8)
            rows = jnp.concatenate([ctx[j, pl.ds(s * HEADS + at, 8), :] for s in steps], axis=0)
            return jnp.concatenate([rows[:, :256], rows[:, 256:]], axis=0).astype(BF16)

        send, recv = sems.take(2)

        def send_group(i, c):
            g = lax.rem(l + i, LOCALS)
            ctx_send[g] = group(g)
            rcopy(ctx_send.at[g], ctx_recv.at[l], send, recv, (n, g)).start()
            return c

        lax.fori_loop(1, LOCALS, send_group, 0)
        ctx_recv[l] = group(l)
        return rcopy(ctx_send.at[others], ctx_recv.at[others], send, recv, here)

    def select(rows, columns, test):
        return jnp.where(test(iota((rows, columns), 0), iota((rows, columns), 1)), 1.0, 0.0).astype(BF16)

    def slots(rows, device):
        lanes = jnp.broadcast_to(slot_v[...], (rows, DEVS)).astype(F32)
        at = device(iota((rows, DEVS), 0)) == iota((rows, DEVS), 1)
        return jnp.sum(jnp.where(at, lanes, 0.0), axis=1, keepdims=True).astype(jnp.int32)

    def chain(j, steps, bufs, sems, context, only):
        count = len(steps)
        rows = LOCALS * count
        bufs = list(bufs)
        take = lambda count=1: [bufs.pop(0) for _ in range(count)]
        ctx_send, ctx_recv, wide, values, part, pair, summed, mixed = take(8)
        got, away, back = take(3)
        gu, sq_send, sq_recv, hidden = take(4)
        gu_bufs = take(8)
        part2, pair2, summed2 = take(3)
        got2 = take()[0]
        last, done = take(2)

        def halves(product, part, pair, summed):
            part[...] = product.reshape(NODES, rows, COLS)
            recv = sems.take(1)[0]
            sems.start(part.at[:, :, pl.ds(theirs, HALF)], pair, recv, sibling)
            yield
            arrived(pair, recv, here)
            summed[...] = (part[:, :, pl.ds(mine, HALF)].astype(F32) + pair[...].astype(F32)).astype(BF16)

        if only:
            loads[2].wait()
        context.wait()
        for t in range(2):
            recv = ctx_recv[:, :, t * 128 : t * 128 + 128].astype(F32)
            for half in range(2):
                for s in range(count):
                    at = (half * count + s) * 8
                    wide[half * 2 + t, s * 128 : s * 128 + 128] = recv[:, at : at + 8].reshape(128, 128)
        for h in range(8):
            head = [wide[t, pl.ds(h, rows, stride=8), :] for t in range(LATENT // 128)]
            head = jnp.concatenate(head, axis=1).astype(BF16)
            values[n, :, h * 128 : h * 128 + 128] = dot(head, wuv[h]).astype(BF16)
        yield from GATHER[VALUES[j]](values, node, sems, here)
        if only:
            loads[3].wait()
        product = dot(values[...].reshape(NODES * rows, 1024), wout[...]).astype(BF16)
        if j == 1:
            pick = select(DEVS, DEVS, lambda row, column: dest_v[...] == row)
            by_step = product.reshape(NODES, count, LOCALS, COLS)
            moved = [dot(pick, by_step[:, s].reshape(DEVS, COLS)).astype(BF16) for s in range(count)]
            product = jnp.concatenate([m.reshape(NODES, LOCALS, COLS) for m in moved], axis=1)
        yield from halves(product, part, pair, summed)

        yield from ring_scatter(summed, got, away, chips, sems, here)
        recv = sems.take(1)[0]
        sems.start(away, back, recv, chips.device(chips.q, chips.r))
        if only:
            loads[4].wait()
        slot = slots(2 * LOCALS, lambda row: chips.r * 2 * LOCALS + row)
        pick = select(
            2 * LOCALS, 4 * LOCALS,
            lambda row, column: (column // 2 == row) & ((lax.rem(column, 2) == slot) == (j == 1)),
        )
        skip = [dot(pick, resid[s, :, pl.ds(mine, HALF)]) for s in steps]
        skip = jnp.concatenate([k.reshape(2, LOCALS, HALF) for k in skip], axis=1)
        yield
        arrived(back, recv, here)
        two = pl.ds(chips.r * 2, 2)
        mixed[core, two] = (skip + (away[...].astype(F32) + back[...].astype(F32))).astype(BF16)

        side = sems.take(1)[0]
        recv = sems.take(3)

        def pass_on(ring):
            ref = mixed.at[core, pl.ds(ring * 2, 2)]
            sems.start(ref, ref, side, sibling)

        for i, ring in enumerate((chips.up, chips.dn, chips.op)):
            ref = mixed.at[core, two]
            sems.start(ref, ref, recv[i], chips.device(chips.p, ring))
        pass_on(chips.r)
        yield
        for i, ring in enumerate((chips.dn, chips.up, chips.op)):
            arrived(mixed.at[core, pl.ds(ring * 2, 2)], recv[i], here)
            pass_on(ring)
        arrived(mixed.at[1 - core], side, here)

        if only:
            loads[5].wait()
            loads[6].wait()
        sq = sems.take(2)

        left = mixed[0].reshape(NODES * rows, HALF).astype(F32)
        right = mixed[1, :, :, HALF - OFFSET :].reshape(NODES * rows, OFFSET).astype(F32)
        whole = jnp.concatenate([left, right], axis=1)
        scaled = (whole * gain_row).astype(BF16)
        gu[:, :, :HID] = dot(scaled, wg[...]).astype(BF16).reshape(NODES, rows, HID)
        gu[:, :, HID:] = dot(scaled, wu[...]).astype(BF16).reshape(NODES, rows, HID)

        def squares():
            square = whole * whole
            lanes = square[:, :128]
            for t in range(1, COLS // 128):
                lanes += square[:, t * 128 : t * 128 + 128]
            sq_send[...] = lax.dot_general(
                jnp.ones((8, 128), F32), lanes, NT, precision=lax.Precision.HIGHEST, preferred_element_type=F32
            )

            def send_sq(i, c):
                p = lax.rem(n + i, NODES)
                rcopy(sq_send, sq_recv.at[n], sq[0], sq[1], (p, l)).start()
                return c

            lax.fori_loop(1, NODES, send_sq, 0)
            sq_recv[n] = sq_send[...]

        yield from scatter8(gu, node, sems, here, squares, *gu_bufs)
        seven = pl.ds(0, NODES - 1)
        rcopy(sq_recv.at[seven], sq_recv.at[seven], sq[0], sq[1], here).wait()
        inverse = lax.rsqrt(jnp.sum(sq_recv[...], axis=0) / D + EPS)
        inverse = jnp.broadcast_to(inverse[:1], (rows, NODES * rows))
        lane = n * rows + iota((rows, NODES * rows), 0)
        inverse = jnp.where(iota((rows, NODES * rows), 1) == lane, inverse, 0.0)
        inverse = jnp.sum(inverse, axis=1, keepdims=True)
        rd, re = gu_bufs[3], gu_bufs[4]
        total = gu[n].astype(F32) + rd[...].astype(F32) + re[0].astype(F32) + re[1].astype(F32)
        total *= inverse
        gate, up = total[:, :HID], total[:, HID:]
        hidden[n] = (gate / (1.0 + jnp.exp(-gate)) * up).astype(BF16)
        yield from GATHER[HIDDEN[j]](hidden, node, sems, here)
        if only:
            loads[7].wait()
        product = dot(hidden[...].reshape(NODES * rows, HID), wd[...]).astype(BF16)
        yield from halves(product, part2, pair2, summed2)
        yield from scatter1(summed2, got2, chip, lambda to: (n, to * 2 + core), sems, here)
        total = jnp.sum(got2[...].astype(F32), axis=0)
        last[core] = (mixed[core, chip].astype(F32) + total).astype(BF16)
        recv = sems.take(1)[0]
        sems.start(last.at[core], last.at[core], recv, sibling)
        yield
        arrived(last.at[1 - core], recv, here)
        done[:, :HALF] = last[0].astype(F32)
        done[:, HALF:] = last[1, :, HALF - OFFSET :].astype(F32)

    both = pl.ds(0, DEVS - 1)
    running = {}

    def begin(j):
        for k, (which, steps) in enumerate(CHAINS):
            if which == j:
                context = send_context(j, steps, bufs[k], sems[k])
                running["abcdef"[k]] = (chain(j, steps, bufs[k], sems[k], context, k == 0), sems[k])

    def advance(name):
        steps, held = running[name]
        held.settle()
        try:
            next(steps)
        except StopIteration:
            del running[name]

    def sort_tiles():
        rcopy(tiles.at[both], r1.at[both], far.at[0], far.at[1], here).wait()

        def sort(o, c):
            s2[o] = r1[dest_s[o]]
            return c

        lax.fori_loop(0, DEVS, sort, 0)

        def deliver(i, c):
            p = lax.rem(me + i, DEVS)
            rcopy(s2.at[p], r2.at[me], far.at[2], far.at[3], (p // LOCALS, lax.rem(p, LOCALS))).start()
            return c

        lax.fori_loop(1, DEVS, deliver, 0)
        r2[me] = s2[me]

    def attend_moved():
        rcopy(s2.at[both], r2.at[both], far.at[2], far.at[3], here).wait()
        for s in range(STEPS):
            for hb in range(blocks):
                for cb in range(5):
                    at = s * HEADS + hb * 16
                    query_arr[at : at + 16, cb * 128 : cb * 128 + 128] = r2[(s * blocks + hb) * 5 + cb]
        for cb in range(5):
            fresh[1, :, cb * 128 : cb * 128 + 128] = r2[STEPS * blocks * 5 + cb]
        attention(1)
        begin(1)

    loads[1].wait()
    for copy in loads[2:]:
        copy.start()
    attention(0)
    pl.semaphore_wait(barrier, NODES - 1 + LOCALS - 1)
    lax.fori_loop(1, LOCALS, greet_all, 0)
    begin(0)
    pl.semaphore_wait(ready, LOCALS - 1)
    lax.fori_loop(1, DEVS, spread, 0)

    for name in ORDER:
        if name == "1":
            sort_tiles()
        elif name == "2":
            attend_moved()
        elif name in running:
            advance(name)
    while running:
        for name in list(running):
            advance(name)

    slot = slots(LOCALS, lambda row: chip * LOCALS + core * 8 + row // 2)
    pick = select(
        LOCALS, LOCALS,
        lambda row, column: (lax.rem(column, 8) == row // 2) & ((lax.rem(row, 2) == slot) == (column >= 8)),
    )
    at = pl.multiple_of(core * 8, 8)
    for s in range(STEPS):
        rows = [
            bufs[k][-1][pl.ds(steps.index(s) * LOCALS + at, 8), :]
            for j in range(2)
            for k, (which, steps) in enumerate(CHAINS)
            if which == j and s in steps
        ]
        out[s] = dot(pick, jnp.concatenate(rows, axis=0).astype(BF16)).astype(BF16)
    for held in sems:
        held.settle()
        held.settle()
        assert held.used <= RECEIVERS and senders.used <= SENDERS


CHAINS = ((0, (0,)), (0, (1,)), (0, (2,)), (1, (0,)), (1, (1,)), (1, (2,)))
SENDERS, RECEIVERS = 51, 29
GATHER = {"three": gather8, "two": gather2}
VALUES = ("three", "three")
HIDDEN = ("three", "two")
ORDER = "abcabc1abc2abcabcdef"


def local(
    cache_pool, block_table, lengths, mig_slot, mig_dest, queries, new_entries, residual,
    w_uv, w_out, norm_gain, w_gate, w_up, w_down,
):
    by_slot = queries.reshape(STEPS * 2, HEADS, WIDTH)
    vm = pl.BlockSpec(memory_space=pltpu.VMEM)
    hbm = pl.BlockSpec(memory_space=pl.ANY)
    smem = pl.BlockSpec(memory_space=pltpu.SMEM)
    dma = pltpu.SemaphoreType.DMA
    V = pltpu.VMEM
    tile = (DEVS, 16, 128)
    return pl.pallas_call(
        kernel,
        out_shape=jax.ShapeDtypeStruct((STEPS, LOCALS, COLS), BF16),
        in_specs=[smem] * 4 + [vm] * 4 + [hbm] * 8,
        out_specs=vm,
        scratch_shapes=[
            V((STEPS * 2, HEADS, WIDTH), BF16), V((4, WIDTH, 256), BF16), V((STEPS, 64, COLS), BF16),
            V((8, LATENT, 128), BF16), V((1024, COLS), BF16), V((COLS, HID), BF16), V((COLS, HID), BF16),
            V((HID, COLS), BF16),
            V(tile, BF16), V(tile, BF16), V(tile, BF16), V(tile, BF16),
            V((STEPS * HEADS, KEYS), BF16), V((2, 16, KEYS), BF16), V((2, STEPS * HEADS, LATENT), F32),
            *[shape for _, steps in CHAINS for shape in chain_shapes(len(steps))],
            dma((8,)), pltpu.SemaphoreType.REGULAR, dma((4,)), dma((SENDERS,)), *[dma((RECEIVERS,)) for _ in CHAINS],
        ],
        compiler_params=pltpu.CompilerParams(
            collective_id=0, has_side_effects=True, vmem_limit_bytes=60 * 2**20
        ),
        name="layer",
    )(
        block_table, lengths, mig_slot, mig_dest, mig_slot.reshape(1, DEVS), mig_dest.reshape(1, DEVS),
        norm_gain, new_entries,
        by_slot, cache_pool, residual, w_uv, w_out, w_gate, w_up, w_down,
    )


def solution(mesh):
    in_specs = (
        P(("node", "local"), None, None),
        P(("node", "local"), None),
        P(),
        P(),
        P(),
        P(None, ("node", "local"), None),
        P(None, ("node", "local"), None),
        P(None, None, "node"),
        P("local", None, None),
        P("local", "node"),
        P("node"),
        P("node", "local"),
        P("node", "local"),
        P("local", "node"),
    )
    out_specs = P(None, "local", "node")
    return jax.shard_map(local, mesh=mesh, in_specs=in_specs, out_specs=out_specs, check_vma=False)
```
